512 devices in a mesh: tm: 16 (over y, core), space: 32 (over x, z).
Axes of the slice: x: 4, y: 8, z: 8, core: 2. Of those that a mesh axis runs over, the one named last changes fastest.
Arguments:
- coupling: bfloat16 [16, 2048, 2048], P('tm', 'space'), may hold values from -0.125 to 0.125
- arrow_link: float32 [16, 2048, 64], P('tm'), may hold values from -0.75 to 0.75
- local_cov: float32 [16, 2048, 2048], P('tm', 'space'), as said below
- boundary_cov: float32 [16, 2048, 2048], P('tm', 'space'), as said below
- boundary_arrow: float32 [16, 2048, 64], P('tm', 'space'), may hold values from -6 to 6
- fixed_cov: float32 [64, 64], replicated, as said below
Outputs:
- diag_blocks: float32 [16, 2048, 2048], P('tm', 'space')
- cross_blocks: float32 [16, 2048, 2048], P('tm', 'space')
- arrow_covs: float32 [16, 2048, 64], P('tm', 'space')
The draws below stay inside these ranges and needn't reach their ends.
Inputs may be any that keep to these rules, and one draw needn't show every extreme that they name: `local_cov`: each block is symmetric. `boundary_cov`: each block is symmetric. `fixed_cov`: symmetric.
All inputs are finite; a program needn't handle non-finite values.
Results may differ from the reference program's by a relative error of at most 0.0003.
Values may be sent and summed in bfloat16 or wider, within the bound.
No kernel may reach another device: no remote copies, remote signals or barrier semaphores. Data moves between devices by JAX's collectives and lax.ppermute only.
A program may use at most 64 MiB of HBM per device.

```python
import math
import jax
import jax.numpy as jnp
from jax import lax

NS = 2048
NF = 64
STEPS = 16


def symmetric_blocks(key, blocks, extent, lowest, largest, spread):
    key_entries, key_diagonal, key_scales = jax.random.split(key, 3)
    normal_part = jax.random.truncated_normal(key_entries, -4.0, 4.0, (blocks, extent, extent), jnp.float32)
    entries = normal_part
    symmetric = (entries + jnp.swapaxes(entries, 1, 2)) * (1.0 / math.sqrt(2.0 * extent))
    diagonal = jax.random.uniform(key_diagonal, (blocks, extent), jnp.float32, lowest, largest)
    identity = jnp.eye(extent, dtype=jnp.float32)
    matrix = symmetric + diagonal[:, :, None] * identity
    scales = jnp.exp(jax.random.uniform(key_scales, (blocks, extent), jnp.float32, 0.0, spread))
    return matrix * scales[:, :, None] * scales[:, None, :]


def draw_local_cov(key, part):
    key = jax.random.fold_in(key, 11)
    return symmetric_blocks(key, STEPS, NS, 1.0, 3.0, 0.0)


def draw_boundary_cov(key, part):
    key = jax.random.fold_in(key, 23)
    return symmetric_blocks(key, STEPS, NS, 1.0, 3.0, 0.0)


def draw_fixed_cov(key, part):
    key = jax.random.fold_in(key, 37)
    return symmetric_blocks(key, 1, NF, 1.0, 3.0, 0.0)[0]


def block_levels(key, dims, shards, least, top_value):
    level, own = 1.0, jax.random.fold_in(key, 6)
    for axis_at, blocks in shards:
        draws = jnp.exp(jax.random.uniform(jax.random.fold_in(own, axis_at), (blocks,), jnp.float32, least / len(shards), top_value / len(shards)))
        level = level * jnp.repeat(draws, dims[axis_at] // blocks).reshape([-1 if axis == axis_at else 1 for axis in range(len(dims))])
    return level


def gaussian(key, shape, width, limit, cuts=(), held_as=jnp.bfloat16):
    array = width * jax.random.normal(key, shape, jnp.float32)
    if cuts:
        array = array * block_levels(key, shape, cuts, -0.22, 0.18)
    return jnp.clip(array, -limit, limit).astype(held_as)


def setup_inputs(seed: int = 0) -> dict:
    key_list = jax.random.split(jax.random.key(seed), 7)
    coupling = gaussian(key_list[0], (STEPS, NS, NS), NS ** -0.5, 0.125, ((0, 16), (1, 32)))
    arrow_link = gaussian(key_list[1], (STEPS, NS, NF), NF ** -0.5, 0.75, ((0, 16),), jnp.float32)
    local_cov = draw_local_cov(jax.random.fold_in(key_list[6], 71), 0)
    boundary_cov = draw_boundary_cov(jax.random.fold_in(key_list[6], 71), 0)
    boundary_arrow = gaussian(key_list[4], (STEPS, NS, NF), 1.0, 6.0, ((0, 16), (1, 32)), jnp.float32)
    fixed_cov = draw_fixed_cov(jax.random.fold_in(key_list[6], 71), 0)
    return {"coupling": coupling, "arrow_link": arrow_link, "local_cov": local_cov, "boundary_cov": boundary_cov, "boundary_arrow": boundary_arrow, "fixed_cov": fixed_cov}


def reference(coupling, arrow_link, local_cov, boundary_cov, boundary_arrow, fixed_cov):
    highest = lax.Precision.HIGHEST
    later_cov = jnp.concatenate([boundary_cov[1:], jnp.zeros((1, NS, NS), jnp.float32)], axis=0)
    later_arrow = jnp.concatenate([boundary_arrow[1:], jnp.zeros((1, NS, NF), jnp.float32)], axis=0)

    def interior_step(operands):
        weights, link_block, local_block, succ_block, succ_arrow = operands
        cross_block = jnp.dot(weights, succ_block, precision=highest, preferred_element_type=jnp.float32)
        cross_block = cross_block + jnp.dot(link_block, succ_arrow.T, precision=highest, preferred_element_type=jnp.float32)
        arrow_cov = jnp.dot(weights, succ_arrow, precision=highest, preferred_element_type=jnp.float32)
        arrow_cov = arrow_cov + jnp.dot(link_block, fixed_cov, precision=highest, preferred_element_type=jnp.float32)
        diag_block = local_block + jnp.dot(weights, cross_block.T, precision=highest, preferred_element_type=jnp.float32)
        diag_block = diag_block + jnp.dot(link_block, arrow_cov.T, precision=highest, preferred_element_type=jnp.float32)
        return diag_block, cross_block, arrow_cov

    diag_blocks, cross_blocks, arrow_covs = lax.map(interior_step, (coupling, arrow_link, local_cov, later_cov, later_arrow))
    return (diag_blocks, cross_blocks, arrow_covs)
```

```python
import jax
import jax.numpy as jnp
from jax import lax
from jax.sharding import Mesh, PartitionSpec as P

F32, F16, BF16 = jnp.float32, jnp.float16, jnp.bfloat16
HIGH = lax.Precision.HIGH


def exponent(largest):
    return jnp.floor(jnp.log2(jnp.clip(largest, 1e-30, 1e38)))


def dot_t(a, b, **kw):
    return lax.dot_general(a, b, (((1,), (1,)), ((), ())), preferred_element_type=F32, **kw)


def two_parts(v, axis):
    top = lax.reduce_precision(v, 8, 7)
    return jnp.concatenate([top.astype(BF16), (v - top).astype(BF16)], axis=axis)


def spread(v, axis):
    n = lax.axis_size(axis)
    return lax.all_to_all(jnp.broadcast_to(v[None], (n,) + v.shape), axis, 0, 0, tiled=True)


def shards(coupling, arrow_link, local_cov, boundary_cov, boundary_arrow, fixed_cov):
    c_own, link, local = coupling[0], arrow_link[0], local_cov[0]
    s_own, a_own = boundary_cov[0], boundary_arrow[0]
    nx, nz = lax.axis_size("x"), lax.axis_size("z")
    steps = lax.axis_size("y") * lax.axis_size("c")
    rows, ns = c_own.shape
    nf = a_own.shape[1]
    ix, iz = lax.axis_index("x"), lax.axis_index("z")

    exp_s = exponent(jnp.max(jnp.abs(s_own), axis=1, keepdims=True))
    exp_a = exponent(jnp.max(jnp.abs(a_own), axis=1, keepdims=True))
    bound = 0.125 * jnp.sum(jnp.abs(s_own), axis=1, keepdims=True)
    bound = bound + 0.75 * jnp.sum(jnp.abs(a_own), axis=1, keepdims=True)
    exp_b = exponent(bound) + 2
    lane = lax.broadcasted_iota(jnp.int32, (rows, nf), 1)
    exps = jnp.where(lane == 0, exp_s, jnp.where(lane == 1, exp_a, exp_b))
    packed = jnp.concatenate(
        [
            (s_own * jnp.exp2(13 - exp_s)).astype(F16),
            (a_own * jnp.exp2(13 - exp_a)).astype(F16),
            exps.astype(F16),
        ],
        axis=1,
    )
    group = nx * nz
    route = [
        (t * group + b, (t - 1) * group + (b % nx) * nz + b // nx)
        for t in range(1, steps)
        for b in range(group)
    ]
    packed = lax.ppermute(packed, ("y", "c", "x", "z"), route)

    c_rows = lax.all_gather(c_own, "z", axis=0, tiled=True)
    link_rows = lax.dynamic_slice_in_dim(link, ix * nz * rows, nz * rows, 0)

    tails = spread(spread(packed[:, ns:], "z"), "x").astype(F32)
    tails = tails.transpose(1, 0, 2, 3).reshape(ns, 2 * nf)
    exp_z = jnp.max(tails[:, nf + 2].reshape(nz, -1), axis=1)
    a_all = tails[:, :nf] * jnp.exp2(tails[:, nf + 1 : nf + 2] - 13)
    arrow2 = jnp.dot(c_own, two_parts(a_all, 1), preferred_element_type=F32)
    link_own = lax.dynamic_slice_in_dim(link, (ix * nz + iz) * rows, rows, 0)
    arrow = arrow2[:, :nf] + arrow2[:, nf:]
    arrow = arrow + jnp.dot(link_own, fixed_cov, precision=lax.Precision.HIGHEST)
    arrows = spread(arrow, "x").reshape(nx * rows, nf)

    succ = spread(packed, "x").reshape(nx * rows, -1).astype(F32)
    s_cols = succ[:, :ns] * jnp.exp2(succ[:, ns + nf : ns + nf + 1] - 13)
    a_cols = succ[:, ns : ns + nf] * jnp.exp2(succ[:, ns + nf + 1 : ns + nf + 2] - 13)
    exp_own = jnp.max(succ[:, ns + nf + 2])
    cross2 = dot_t(c_rows, two_parts(s_cols, 0))
    cross = cross2[:, : nx * rows] + cross2[:, nx * rows :]
    cross = cross + dot_t(link_rows, a_cols, precision=HIGH)
    cross = (cross * jnp.exp2(14 - exp_own)).astype(F16)
    cross = cross.reshape(nz, rows, nx * rows)
    cross = lax.all_to_all(cross, "z", 0, 0, tiled=True)
    scale = jnp.exp2(exp_z - 14)[:, None, None]
    cross_rows = (cross.astype(F32) * scale).transpose(1, 0, 2).reshape(rows, ns)

    cross_all = spread(cross, "x").astype(F32) * scale[None]
    cross_all = cross_all.transpose(0, 2, 1, 3).reshape(nx * rows, ns)
    diag2 = dot_t(two_parts(cross_all, 0), c_rows)
    diag = diag2[: nx * rows] + diag2[nx * rows :]
    diag = diag + dot_t(arrows, link_rows, precision=HIGH)
    diag = lax.all_to_all(diag.reshape(nx, rows, nz * rows), "x", 0, 0, tiled=True)
    diag_rows = local + diag.transpose(1, 0, 2).reshape(rows, ns)
    return (diag_rows[None], cross_rows[None], arrow[None])


def solution(mesh):
    mesh = Mesh(mesh.devices.reshape(8, 2, 4, 8), ("y", "c", "x", "z"))
    step, space = ("y", "c"), ("x", "z")
    row_split = P(step, space, None)
    return jax.shard_map(
        shards,
        mesh=mesh,
        in_specs=(row_split, P(step, None, None), row_split, row_split, row_split, P()),
        out_specs=(row_split, row_split, row_split),
        check_vma=False,
    )
```

```python
import jax
import jax.numpy as jnp
from jax import lax
from jax.sharding import Mesh, PartitionSpec as P

F32, F16, BF16 = jnp.float32, jnp.float16, jnp.bfloat16
HIGH = lax.Precision.HIGH


def exponent(largest):
    return jnp.floor(jnp.log2(jnp.clip(largest, 1e-30, 1e38)))


def dot_t(a, b, **kw):
    return lax.dot_general(a, b, (((1,), (1,)), ((), ())), preferred_element_type=F32, **kw)


def two_parts(v):
    top = lax.reduce_precision(v, 8, 7)
    return top.astype(BF16), (v - top).astype(BF16)


def spread(v, axis):
    n = lax.axis_size(axis)
    return lax.all_to_all(jnp.broadcast_to(v[None], (n,) + v.shape), axis, 0, 0, tiled=True)


def passed(v, axis, by):
    n = lax.axis_size(axis)
    return lax.ppermute(v, axis, [(i, (i + by) % n) for i in range(n)])


def shards(coupling, arrow_link, local_cov, boundary_cov, boundary_arrow, fixed_cov):
    c_own, link, local = coupling[0], arrow_link[0], local_cov[0]
    s_own, a_own = boundary_cov[0], boundary_arrow[0]
    nx, nz = lax.axis_size("x"), lax.axis_size("z")
    steps = lax.axis_size("y") * lax.axis_size("c")
    group = nx * nz
    rows, ns = c_own.shape
    nf = a_own.shape[1]
    cols = nx * rows
    ix, iz = lax.axis_index("x"), lax.axis_index("z")

    route = []
    for t in range(1, steps):
        for x in range(nx):
            for z in range(nz):
                target = (x - x % 2 + z % 2) * nz + z - z % 2 + x % 2
                route.append((t * group + x * nz + z, (t - 1) * group + target))
    bound_a = jnp.max(jnp.abs(a_own), axis=1, keepdims=True)
    bound = 0.125 * jnp.sum(jnp.abs(s_own), axis=1, keepdims=True) + 0.75 * nf * bound_a
    lane = lax.broadcasted_iota(jnp.int32, (rows, nf), 1)
    exps = jnp.where(lane == 0, exponent(bound) + 2, exponent(0.125 * cols * bound_a) + 2)
    exps = exps.astype(BF16)
    s_top, s_low = two_parts(s_own)
    a_top, a_low = two_parts(a_own)
    packed = jnp.stack(
        [
            jnp.concatenate([s_top, a_top, exps], axis=1),
            jnp.concatenate([s_low, a_low, exps], axis=1),
        ]
    )
    packed = lax.ppermute(packed, ("y", "c", "x", "z"), route)
    before, after = passed(packed, "x", 1), passed(packed, "x", -1)
    far_top, far_low = passed(packed[0], "x", 2), passed(packed[1], "x", -2)
    succ = jnp.zeros((nx,) + packed.shape, BF16)
    for by, block in ((0, packed), (nx - 1, before), (1, after)):
        succ = lax.dynamic_update_index_in_dim(succ, block, (ix + by) % nx, 0)
    far = jnp.stack([far_top, far_low])
    succ = lax.dynamic_update_index_in_dim(succ, far, (ix + 2) % nx, 0)
    succ = succ.transpose(1, 0, 2, 3)
    s_cols = succ[..., :ns].reshape(2 * cols, ns)
    a_two = succ[..., ns : ns + nf].reshape(2, cols, nf)
    exps = jnp.max(succ[0, :, :, ns + nf : ns + nf + 2].astype(F32), axis=(0, 1))

    link_rows = lax.dynamic_slice_in_dim(link, ix * nz * rows, nz * rows, 0)
    arrow_term = dot_t(link_rows, a_two[0].astype(F32) + a_two[1].astype(F32), precision=HIGH)
    place = a_two.reshape(2, nx // 2, 1, 1, 2, rows, nf)
    here = lax.broadcasted_iota(jnp.int32, (2, nz // 2), 0) == iz % 2
    here &= lax.broadcasted_iota(jnp.int32, (2, nz // 2), 1) == iz // 2
    place = jnp.where(here[None, None, :, :, None, None, None], place, jnp.zeros((), BF16))
    place = place.reshape(2, ns, nf)
    place = jnp.concatenate([place[0], place[1]], axis=1)
    s_cols, arrow_term, place = lax.optimization_barrier((s_cols, arrow_term, place))

    c_rows = spread(c_own, "z").reshape(nz * rows, ns)

    cross2 = dot_t(c_rows, s_cols)
    cross = (cross2[:, :cols] + cross2[:, cols:] + arrow_term) * jnp.exp2(14 - exps[0])
    share2 = jnp.dot(c_rows, place, preferred_element_type=F32)
    share = (share2[:, :nf] + share2[:, nf:]) * jnp.exp2(14 - exps[1])
    lane = lax.broadcasted_iota(jnp.int32, (nz * rows, nf), 1)
    marks = jnp.where(lane == 0, exps[0], exps[1])
    sent = jnp.concatenate([cross.astype(F16), share.astype(F16), marks.astype(F16)], axis=1)
    sent = lax.all_to_all(sent.reshape(nz, rows, -1), "z", 0, 0, tiled=True)
    cross = sent[..., :cols]
    marks = sent[:, :1, cols + nf : cols + nf + 2].astype(F32)
    scale = jnp.exp2(marks[..., :1] - 14)

    every = spread(cross, "x").astype(F32) * scale[None]
    every = every.transpose(0, 2, 1, 3).reshape(cols, ns)
    runs = []
    for z in range(nz):
        for q in range(nx // 2):
            first = (2 * q + z % 2) * nz * rows + z // 2 * 2 * rows
            runs.append(c_rows[:, first : first + 2 * rows])
    c_turned = lax.optimization_barrier(jnp.concatenate(runs, axis=1))
    diag2 = dot_t(jnp.concatenate(two_parts(every), axis=0), c_turned)
    diag = (diag2[:cols] + diag2[cols:]).reshape(nx, rows, nz * rows)
    diag = lax.all_to_all(diag, "x", 0, 0, tiled=True)

    own = cross.astype(F32) * scale
    pieces = []
    for x in range(nx):
        for k in range(nz // 2):
            half = slice(x // 2 * 2 * rows, (x // 2 + 1) * 2 * rows)
            pieces.append(own[2 * k + x % 2, :, half])
    cross_rows = jnp.concatenate(pieces, axis=1)
    share = sent[..., cols : cols + nf].astype(F32) * jnp.exp2(marks[..., 1:] - 14)
    link_own = lax.dynamic_slice_in_dim(link, (ix * nz + iz) * rows, rows, 0)
    arrow = jnp.dot(link_own, fixed_cov, precision=lax.Precision.HIGHEST)
    arrow = jnp.sum(share, axis=0) + arrow
    local = lax.optimization_barrier(local + dot_t(arrow, link, precision=HIGH))
    diag_rows = local + diag.transpose(1, 0, 2).reshape(rows, ns)
    return (diag_rows[None], cross_rows[None], arrow[None])


def solution(mesh):
    mesh = Mesh(mesh.devices.reshape(8, 2, 4, 8), ("y", "c", "x", "z"))
    step, space = ("y", "c"), ("x", "z")
    row_split = P(step, space, None)
    return jax.shard_map(
        shards,
        mesh=mesh,
        in_specs=(row_split, P(step, None, None), row_split, row_split, row_split, P()),
        out_specs=(row_split, row_split, row_split),
        check_vma=False,
    )
```

```python
import functools

import jax
import jax.numpy as jnp
from jax import lax
from jax.experimental import pallas as pl
from jax.experimental.pallas import tpu as pltpu
from jax.sharding import Mesh, PartitionSpec as P

F32, F16, BF16 = jnp.float32, jnp.float16, jnp.bfloat16
HIGH = lax.Precision.HIGH


def exponent(largest):
    return jnp.floor(jnp.log(jnp.clip(largest, 1e-30, 1e38)) * 1.4426950408889634)


def dot_t(a, b, **kw):
    return lax.dot_general(a, b, (((1,), (1,)), ((), ())), preferred_element_type=F32, **kw)


def two_parts(v):
    top = lax.reduce_precision(v, 8, 7)
    return top.astype(BF16), (v - top).astype(BF16)


def spread(v, axis):
    n = lax.axis_size(axis)
    return lax.all_to_all(jnp.broadcast_to(v[None], (n,) + v.shape), axis, 0, 0, tiled=True)


def passed(v, axis, by):
    n = lax.axis_size(axis)
    return lax.ppermute(v, axis, [(i, (i + by) % n) for i in range(n)])


def halves(first, second):
    lane = lax.broadcasted_iota(jnp.int32, first.shape, 1)
    low = jnp.where(lane < 64, first, pltpu.roll(second, 64, 1))
    high = jnp.where(lane < 64, pltpu.roll(first, 64, 1), second)
    return low, high


def pack_kernel(nx, nz, c_ref, s_ref, a_ref, copies_ref, packed_ref):
    rows, ns = s_ref.shape
    nf = a_ref.shape[1]
    run = 2 * rows

    def put(at, value):
        top = value.astype(BF16)
        packed_ref[0, :, at : at + value.shape[1]] = top
        low = (value - top.astype(F32)).astype(BF16)
        packed_ref[1, :, at : at + value.shape[1]] = low

    total = jnp.zeros((rows, run), F32)
    for q in range(nx // 2):
        for k in range(nz // 2):
            first = slice((2 * q * nz // 2 + k) * run, (2 * q * nz // 2 + k + 1) * run)
            second = slice(first.start + nz // 2 * run, first.stop + nz // 2 * run)
            pair = s_ref[:, first], s_ref[:, second]
            total = total + jnp.abs(pair[0]) + jnp.abs(pair[1])
            for h, value in enumerate(halves(*pair)):
                put(((2 * k + h) * nx // 2 + q) * run, value)
            pair = c_ref[:, first].astype(F32), c_ref[:, second].astype(F32)
            for h, value in enumerate(halves(*pair)):
                at = ((2 * k + h) * nx // 2 + q) * run
                value = value.astype(BF16)
                for z in range(nz):
                    copies_ref[z, :, at : at + run] = value
    a_own = a_ref[...]
    bound_a = jnp.max(jnp.abs(a_own), axis=1, keepdims=True)
    bound = 0.125 * jnp.sum(total, axis=1, keepdims=True) + 0.75 * nf * bound_a
    lane = lax.broadcasted_iota(jnp.int32, (rows, nf), 1)
    exps = jnp.where(lane == 0, exponent(bound), exponent(0.125 * nx * rows * bound_a)) + 2
    put(ns, jnp.concatenate([a_own, exps], axis=1))


def natural_kernel(nx, nz, in_ref, out_ref):
    rows = out_ref.shape[0]
    run = 2 * rows
    for q in range(nx // 2):
        for k in range(nz // 2):
            cut = slice(q * run, (q + 1) * run)
            pair = halves(in_ref[2 * k, :, cut], in_ref[2 * k + 1, :, cut])
            for h, value in enumerate(pair):
                at = ((2 * q + h) * nz // 2 + k) * run
                out_ref[:, at : at + run] = value


def shards(coupling, arrow_link, local_cov, boundary_cov, boundary_arrow, fixed_cov):
    c_own, link, local = coupling[0], arrow_link[0], local_cov[0]
    s_own, a_own = boundary_cov[0], boundary_arrow[0]
    nx, nz = lax.axis_size("x"), lax.axis_size("z")
    steps = lax.axis_size("y") * lax.axis_size("c")
    group = nx * nz
    rows, ns = c_own.shape
    nf = a_own.shape[1]
    cols = nx * rows
    ix, iz = lax.axis_index("x"), lax.axis_index("z")

    copies, packed = pl.pallas_call(
        functools.partial(pack_kernel, nx, nz),
        out_shape=(
            jax.ShapeDtypeStruct((nz, rows, ns), BF16),
            jax.ShapeDtypeStruct((2, rows, ns + 2 * nf), BF16),
        ),
        compiler_params=pltpu.CompilerParams(vmem_limit_bytes=32 << 20),
    )(c_own, s_own, a_own)
    route = [(t * group + b, (t - 1) * group + b) for t in range(1, steps) for b in range(group)]
    packed = lax.ppermute(packed, ("y", "c", "x", "z"), route)
    before, after = passed(packed, "x", 1), passed(packed, "x", -1)
    far_top, far_low = passed(packed[0], "x", 2), passed(packed[1], "x", -2)
    succ = jnp.zeros((nx,) + packed.shape, BF16)
    for by, block in ((0, packed), (nx - 1, before), (1, after)):
        succ = lax.dynamic_update_index_in_dim(succ, block, (ix + by) % nx, 0)
    far = jnp.stack([far_top, far_low])
    succ = lax.dynamic_update_index_in_dim(succ, far, (ix + 2) % nx, 0)
    succ = succ.transpose(1, 0, 2, 3)
    s_cols = succ[..., :ns].reshape(2 * cols, ns)
    a_two = succ[..., ns : ns + nf].reshape(2, cols, nf)
    exps = jnp.max(succ[0, :, :, ns + nf : ns + nf + 2].astype(F32), axis=(0, 1))

    link_rows = lax.dynamic_slice_in_dim(link, ix * nz * rows, nz * rows, 0)
    arrow_term = dot_t(link_rows, a_two[0].astype(F32) + a_two[1].astype(F32), precision=HIGH)
    place = jnp.concatenate([a_two[0], a_two[1]], axis=1)
    s_cols, arrow_term, place = lax.optimization_barrier((s_cols, arrow_term, place))

    c_rows = lax.all_to_all(copies, "z", 0, 0, tiled=True).reshape(nz * rows, ns)

    cross2 = dot_t(c_rows, s_cols)
    cross = (cross2[:, :cols] + cross2[:, cols:] + arrow_term) * jnp.exp2(14 - exps[0])
    c_here = lax.dynamic_slice_in_dim(c_rows, iz * cols, cols, 1)
    share2 = jnp.dot(c_here, place, preferred_element_type=F32)
    share = (share2[:, :nf] + share2[:, nf:]) * jnp.exp2(14 - exps[1])
    lane = lax.broadcasted_iota(jnp.int32, (nz * rows, nf), 1)
    marks = jnp.where(lane == 0, exps[0], exps[1])
    sent = jnp.concatenate([cross.astype(F16), share.astype(F16), marks.astype(F16)], axis=1)
    sent = lax.all_to_all(sent.reshape(nz, rows, -1), "z", 0, 0, tiled=True)
    cross = sent[..., :cols]
    marks = sent[:, :1, cols + nf : cols + nf + 2].astype(F32)
    scale = jnp.exp2(marks[..., :1] - 14)

    every = spread(cross, "x").astype(F32) * scale[None]
    every = every.transpose(0, 2, 1, 3).reshape(cols, ns)
    diag2 = dot_t(jnp.concatenate(two_parts(every), axis=0), c_rows)
    diag = (diag2[:cols] + diag2[cols:]).reshape(nx, rows, nz * rows)
    diag = lax.all_to_all(diag, "x", 0, 0, tiled=True)

    cross_rows = pl.pallas_call(
        functools.partial(natural_kernel, nx, nz),
        out_shape=jax.ShapeDtypeStruct((rows, ns), F32),
    )(cross.astype(F32) * scale)
    share = sent[..., cols : cols + nf].astype(F32) * jnp.exp2(marks[..., 1:] - 14)
    link_own = lax.dynamic_slice_in_dim(link, (ix * nz + iz) * rows, rows, 0)
    arrow = jnp.dot(link_own, fixed_cov, precision=lax.Precision.HIGHEST)
    arrow = jnp.sum(share, axis=0) + arrow
    local = lax.optimization_barrier(local + dot_t(arrow, link, precision=HIGH))
    diag_rows = local + diag.transpose(1, 0, 2).reshape(rows, ns)
    return (diag_rows[None], cross_rows[None], arrow[None])


def solution(mesh):
    mesh = Mesh(mesh.devices.reshape(8, 2, 4, 8), ("y", "c", "x", "z"))
    step, space = ("y", "c"), ("x", "z")
    row_split = P(step, space, None)
    return jax.shard_map(
        shards,
        mesh=mesh,
        in_specs=(row_split, P(step, None, None), row_split, row_split, row_split, P()),
        out_specs=(row_split, row_split, row_split),
        check_vma=False,
    )
```

```python
import functools

import jax
import jax.numpy as jnp
from jax import lax
from jax.experimental import pallas as pl
from jax.experimental.pallas import tpu as pltpu
from jax.sharding import Mesh, PartitionSpec as P

F32, F16, BF16 = jnp.float32, jnp.float16, jnp.bfloat16
HIGH = lax.Precision.HIGH


def exponent(largest):
    return jnp.floor(jnp.log(jnp.clip(largest, 1e-30, 1e38)) * 1.4426950408889634)


def dot_t(a, b, **kw):
    return lax.dot_general(a, b, (((1,), (1,)), ((), ())), preferred_element_type=F32, **kw)


def two_parts(v):
    top = lax.reduce_precision(v, 8, 7)
    return top.astype(BF16), (v - top).astype(BF16)


def spread(v, axis):
    n = lax.axis_size(axis)
    return lax.all_to_all(jnp.broadcast_to(v[None], (n,) + v.shape), axis, 0, 0, tiled=True)


def passed(v, axis, by):
    n = lax.axis_size(axis)
    return lax.ppermute(v, axis, [(i, (i + by) % n) for i in range(n)])


def halves(first, second):
    lane = lax.broadcasted_iota(jnp.int32, first.shape, 1)
    low = jnp.where(lane < 64, first, pltpu.roll(second, 64, 1))
    high = jnp.where(lane < 64, pltpu.roll(first, 64, 1), second)
    return low, high


def pack_kernel(nx, nz, c_ref, s_ref, a_ref, turned_ref, packed_ref):
    rows, ns = s_ref.shape
    nf = a_ref.shape[1]
    run = 2 * rows

    def put(at, value):
        top = value.astype(BF16)
        packed_ref[0, :, at : at + value.shape[1]] = top
        low = (value - top.astype(F32)).astype(BF16)
        packed_ref[1, :, at : at + value.shape[1]] = low

    total = jnp.zeros((rows, run), F32)
    for q in range(nx // 2):
        for k in range(nz // 2):
            first = slice((2 * q * nz // 2 + k) * run, (2 * q * nz // 2 + k + 1) * run)
            second = slice(first.start + nz // 2 * run, first.stop + nz // 2 * run)
            pair = s_ref[:, first], s_ref[:, second]
            total = total + jnp.abs(pair[0]) + jnp.abs(pair[1])
            for h, value in enumerate(halves(*pair)):
                put(((2 * k + h) * nx // 2 + q) * run, value)
            pair = c_ref[:, first].astype(F32), c_ref[:, second].astype(F32)
            for h, value in enumerate(halves(*pair)):
                at = ((2 * k + h) * nx // 2 + q) * run
                turned_ref[:, at : at + run] = value.astype(BF16)
    a_own = a_ref[...]
    bound_a = jnp.max(jnp.abs(a_own), axis=1, keepdims=True)
    bound = 0.125 * jnp.sum(total, axis=1, keepdims=True) + 0.75 * nf * bound_a
    lane = lax.broadcasted_iota(jnp.int32, (rows, nf), 1)
    exps = jnp.where(lane == 0, exponent(bound), exponent(0.125 * nx * rows * bound_a)) + 2
    put(ns, jnp.concatenate([a_own, exps], axis=1))


def natural_kernel(nx, nz, in_ref, out_ref):
    rows = out_ref.shape[0]
    run = 2 * rows
    for q in range(nx // 2):
        for k in range(nz // 2):
            cut = slice(q * run, (q + 1) * run)
            pair = halves(in_ref[2 * k, :, cut], in_ref[2 * k + 1, :, cut])
            for h, value in enumerate(pair):
                at = ((2 * q + h) * nz // 2 + k) * run
                out_ref[:, at : at + run] = value


def shards(coupling, arrow_link, local_cov, boundary_cov, boundary_arrow, fixed_cov):
    c_own, link, local = coupling[0], arrow_link[0], local_cov[0]
    s_own, a_own = boundary_cov[0], boundary_arrow[0]
    nx, nz = lax.axis_size("x"), lax.axis_size("z")
    steps = lax.axis_size("y") * lax.axis_size("c")
    group = nx * nz
    rows, ns = c_own.shape
    nf = a_own.shape[1]
    cols = nx * rows
    ix, iz = lax.axis_index("x"), lax.axis_index("z")

    turned, packed = pl.pallas_call(
        functools.partial(pack_kernel, nx, nz),
        out_shape=(
            jax.ShapeDtypeStruct((rows, ns), BF16),
            jax.ShapeDtypeStruct((2, rows, ns + 2 * nf), BF16),
        ),
        compiler_params=pltpu.CompilerParams(vmem_limit_bytes=32 << 20),
    )(c_own, s_own, a_own)
    route = [(t * group + b, (t - 1) * group + b) for t in range(1, steps) for b in range(group)]
    packed = lax.ppermute(packed, ("y", "c", "x", "z"), route)
    succ = spread(packed, "x")
    succ = succ.transpose(1, 0, 2, 3)
    s_cols = succ[..., :ns].reshape(2 * cols, ns)
    a_two = succ[..., ns : ns + nf].reshape(2, cols, nf)
    exps = jnp.max(succ[0, :, :, ns + nf : ns + nf + 2].astype(F32), axis=(0, 1))

    link_rows = lax.dynamic_slice_in_dim(link, ix * nz * rows, nz * rows, 0)
    arrow_term = dot_t(link_rows, a_two[0].astype(F32) + a_two[1].astype(F32), precision=HIGH)
    place = jnp.concatenate([a_two[0], a_two[1]], axis=1)
    s_cols, arrow_term, place = lax.optimization_barrier((s_cols, arrow_term, place))

    up1, down1 = passed(turned, "z", -1), passed(turned, "z", 1)
    up2, down2 = passed(turned, "z", -2), passed(turned, "z", 2)
    up3, down3 = passed(up2, "z", -1), passed(down2, "z", 1)
    far_up = passed(up2[: rows // 2], "z", -2)
    far_down = passed(down2[rows // 2 :], "z", 2)
    c_rows = jnp.zeros((nz, rows, ns), BF16)
    blocks = ((0, turned), (1, up1), (-1, down1), (2, up2), (-2, down2), (3, up3), (-3, down3))
    for by, block in blocks:
        c_rows = lax.dynamic_update_index_in_dim(c_rows, block, (iz + by) % nz, 0)
    far = jnp.concatenate([far_up, far_down], axis=0)
    c_rows = lax.dynamic_update_index_in_dim(c_rows, far, (iz + nz // 2) % nz, 0)
    c_rows = c_rows.reshape(nz * rows, ns)

    cross2 = dot_t(c_rows, s_cols)
    cross = (cross2[:, :cols] + cross2[:, cols:] + arrow_term) * jnp.exp2(14 - exps[0])
    c_here = lax.dynamic_slice_in_dim(c_rows, iz * cols, cols, 1)
    share2 = jnp.dot(c_here, place, preferred_element_type=F32)
    share = (share2[:, :nf] + share2[:, nf:]) * jnp.exp2(14 - exps[1])
    lane = lax.broadcasted_iota(jnp.int32, (nz * rows, nf), 1)
    marks = jnp.where(lane == 0, exps[0], exps[1])
    sent = jnp.concatenate([cross.astype(F16), share.astype(F16), marks.astype(F16)], axis=1)
    sent = lax.all_to_all(sent.reshape(nz, rows, -1), "z", 0, 0, tiled=True)
    cross = sent[..., :cols]
    marks = sent[:, :1, cols + nf : cols + nf + 2].astype(F32)
    scale = jnp.exp2(marks[..., :1] - 14)

    every = spread(cross, "x").astype(F32) * scale[None]
    every = every.transpose(0, 2, 1, 3).reshape(cols, ns)
    diag2 = dot_t(jnp.concatenate(two_parts(every), axis=0), c_rows)
    diag = (diag2[:cols] + diag2[cols:]).reshape(nx, rows, nz * rows)
    diag = lax.all_to_all(diag, "x", 0, 0, tiled=True)

    cross_rows = pl.pallas_call(
        functools.partial(natural_kernel, nx, nz),
        out_shape=jax.ShapeDtypeStruct((rows, ns), F32),
    )(cross.astype(F32) * scale)
    share = sent[..., cols : cols + nf].astype(F32) * jnp.exp2(marks[..., 1:] - 14)
    link_own = lax.dynamic_slice_in_dim(link, (ix * nz + iz) * rows, rows, 0)
    arrow = jnp.dot(link_own, fixed_cov, precision=lax.Precision.HIGHEST)
    arrow = jnp.sum(share, axis=0) + arrow
    local = lax.optimization_barrier(local + dot_t(arrow, link, precision=HIGH))
    diag_rows = local + diag.transpose(1, 0, 2).reshape(rows, ns)
    return (diag_rows[None], cross_rows[None], arrow[None])


def solution(mesh):
    mesh = Mesh(mesh.devices.reshape(8, 2, 4, 8), ("y", "c", "x", "z"))
    step, space = ("y", "c"), ("x", "z")
    row_split = P(step, space, None)
    return jax.shard_map(
        shards,
        mesh=mesh,
        in_specs=(row_split, P(step, None, None), row_split, row_split, row_split, P()),
        out_specs=(row_split, row_split, row_split),
        check_vma=False,
    )
```

```python
import functools

import jax
import jax.numpy as jnp
from jax import lax
from jax.experimental import pallas as pl
from jax.experimental.pallas import tpu as pltpu
from jax.sharding import Mesh, PartitionSpec as P

F32, F16, BF16 = jnp.float32, jnp.float16, jnp.bfloat16
HIGH = lax.Precision.HIGH


def exponent(largest):
    return jnp.floor(jnp.log(jnp.clip(largest, 1e-30, 1e38)) * 1.4426950408889634)


def dot_t(a, b, **kw):
    return lax.dot_general(a, b, (((1,), (1,)), ((), ())), preferred_element_type=F32, **kw)


def two_parts(v):
    top = lax.reduce_precision(v, 8, 7)
    return top.astype(BF16), (v - top).astype(BF16)


def spread(v, axis):
    n = lax.axis_size(axis)
    return lax.all_to_all(jnp.broadcast_to(v[None], (n,) + v.shape), axis, 0, 0, tiled=True)


def halves(first, second):
    lane = lax.broadcasted_iota(jnp.int32, first.shape, 1)
    low = jnp.where(lane < 64, first, pltpu.roll(second, 64, 1))
    high = jnp.where(lane < 64, pltpu.roll(first, 64, 1), second)
    return low, high


def pack_kernel(cols, s_ref, a_ref, packed_ref):
    rows, ns = s_ref.shape
    nf = a_ref.shape[1]

    def put(at, value):
        top = value.astype(BF16)
        packed_ref[0, :, at : at + value.shape[1]] = top
        low = (value - top.astype(F32)).astype(BF16)
        packed_ref[1, :, at : at + value.shape[1]] = low

    total = jnp.zeros((rows, 128), F32)
    for at in range(0, ns, 128):
        value = s_ref[:, at : at + 128]
        total = total + jnp.abs(value)
        put(at, value)
    a_own = a_ref[...]
    bound_a = jnp.max(jnp.abs(a_own), axis=1, keepdims=True)
    bound = 0.125 * jnp.sum(total, axis=1, keepdims=True) + 0.75 * nf * bound_a
    lane = lax.broadcasted_iota(jnp.int32, (rows, nf), 1)
    exps = jnp.where(lane == 0, exponent(bound), exponent(0.125 * cols * bound_a)) + 2
    put(ns, jnp.concatenate([a_own, exps], axis=1))


def turn_kernel(nx, nz, in_ref, out_ref):
    run = 128

    @pl.loop(0, in_ref.shape[0] // 64)
    def _(step):
        at_rows = pl.ds(pl.multiple_of(step * 64, 64), 64)
        for q in range(nx // 2):
            for k in range(nz // 2):
                first = (q * nz + k) * run
                second = first + nz // 2 * run
                pair = halves(
                    in_ref[at_rows, first : first + run].astype(F32),
                    in_ref[at_rows, second : second + run].astype(F32),
                )
                for h, value in enumerate(pair):
                    at = ((2 * k + h) * nx // 2 + q) * run
                    out_ref[at_rows, at : at + run] = value.astype(BF16)


def natural_kernel(nx, nz, in_ref, out_ref):
    rows = out_ref.shape[0]
    run = 2 * rows
    for q in range(nx // 2):
        for k in range(nz // 2):
            cut = slice(q * run, (q + 1) * run)
            pair = halves(in_ref[2 * k, :, cut], in_ref[2 * k + 1, :, cut])
            for h, value in enumerate(pair):
                at = ((2 * q + h) * nz // 2 + k) * run
                out_ref[:, at : at + run] = value


def shards(coupling, arrow_link, local_cov, boundary_cov, boundary_arrow, fixed_cov):
    c_own, link, local = coupling[0], arrow_link[0], local_cov[0]
    s_own, a_own = boundary_cov[0], boundary_arrow[0]
    nx, nz = lax.axis_size("x"), lax.axis_size("z")
    steps = lax.axis_size("y") * lax.axis_size("c")
    group = nx * nz
    rows, ns = c_own.shape
    nf = a_own.shape[1]
    cols = nx * rows
    ix, iz = lax.axis_index("x"), lax.axis_index("z")

    packed = pl.pallas_call(
        functools.partial(pack_kernel, cols),
        out_shape=jax.ShapeDtypeStruct((2, rows, ns + 2 * nf), BF16),
    )(s_own, a_own)
    route = [(t * group + b, (t - 1) * group + b) for t in range(1, steps) for b in range(group)]
    packed = lax.ppermute(packed, ("y", "c", "x", "z"), route)
    succ = spread(packed, "x")
    succ = succ.transpose(1, 0, 2, 3)
    s_cols = succ[..., :ns].reshape(2 * cols, ns)
    a_two = succ[..., ns : ns + nf].reshape(2, cols, nf)
    exps = jnp.max(succ[0, :, :, ns + nf : ns + nf + 2].astype(F32), axis=(0, 1))

    link_rows = lax.dynamic_slice_in_dim(link, ix * nz * rows, nz * rows, 0)
    arrow_term = dot_t(link_rows, a_two[0].astype(F32) + a_two[1].astype(F32), precision=HIGH)
    place = jnp.concatenate([a_two[0], a_two[1]], axis=1).reshape(nx, 1, rows, 2 * nf)
    here = lax.broadcasted_iota(jnp.int32, (1, nz, 1, 1), 1) == iz
    place = jnp.where(here, place, jnp.zeros((), BF16)).reshape(ns, 2 * nf)
    s_cols, arrow_term, place = lax.optimization_barrier((s_cols, arrow_term, place))

    c_rows = lax.all_gather(c_own, "z", axis=0, tiled=True)
    c_turned = pl.pallas_call(
        functools.partial(turn_kernel, nx, nz),
        out_shape=jax.ShapeDtypeStruct(c_rows.shape, BF16),
        cost_estimate=pl.CostEstimate(flops=0, bytes_accessed=20 << 20, transcendentals=0),
        compiler_params=pltpu.CompilerParams(vmem_limit_bytes=16 << 20),
    )(c_rows)

    cross2 = dot_t(c_rows, s_cols)
    cross = (cross2[:, :cols] + cross2[:, cols:] + arrow_term) * jnp.exp2(14 - exps[0])
    share2 = jnp.dot(c_rows, place, preferred_element_type=F32)
    share = (share2[:, :nf] + share2[:, nf:]) * jnp.exp2(14 - exps[1])
    lane = lax.broadcasted_iota(jnp.int32, (nz * rows, nf), 1)
    marks = jnp.where(lane == 0, exps[0], exps[1])
    sent = jnp.concatenate([cross.astype(F16), share.astype(F16), marks.astype(F16)], axis=1)
    sent = lax.all_to_all(sent.reshape(nz, rows, -1), "z", 0, 0, tiled=True)
    cross = sent[..., :cols]
    marks = sent[:, :1, cols + nf : cols + nf + 2].astype(F32)
    scale = jnp.exp2(marks[..., :1] - 14)

    every = spread(cross, "x").astype(F32) * scale[None]
    every = every.transpose(0, 2, 1, 3).reshape(cols, ns)
    diag2 = dot_t(jnp.concatenate(two_parts(every), axis=0), c_turned)
    diag = (diag2[:cols] + diag2[cols:]).reshape(nx, rows, nz * rows)
    diag = lax.all_to_all(diag, "x", 0, 0, tiled=True)

    cross_rows = pl.pallas_call(
        functools.partial(natural_kernel, nx, nz),
        out_shape=jax.ShapeDtypeStruct((rows, ns), F32),
    )(cross.astype(F32) * scale)
    share = sent[..., cols : cols + nf].astype(F32) * jnp.exp2(marks[..., 1:] - 14)
    link_own = lax.dynamic_slice_in_dim(link, (ix * nz + iz) * rows, rows, 0)
    arrow = jnp.dot(link_own, fixed_cov, precision=lax.Precision.HIGHEST)
    arrow = jnp.sum(share, axis=0) + arrow
    local = lax.optimization_barrier(local + dot_t(arrow, link, precision=HIGH))
    diag_rows = local + diag.transpose(1, 0, 2).reshape(rows, ns)
    return (diag_rows[None], cross_rows[None], arrow[None])


def solution(mesh):
    mesh = Mesh(mesh.devices.reshape(8, 2, 4, 8), ("y", "c", "x", "z"))
    step, space = ("y", "c"), ("x", "z")
    row_split = P(step, space, None)
    return jax.shard_map(
        shards,
        mesh=mesh,
        in_specs=(row_split, P(step, None, None), row_split, row_split, row_split, P()),
        out_specs=(row_split, row_split, row_split),
        check_vma=False,
    )
```

```python
import functools

import jax
import jax.numpy as jnp
from jax import lax
from jax.experimental import pallas as pl
from jax.experimental.pallas import tpu as pltpu
from jax.sharding import Mesh, PartitionSpec as P

F32, F16, BF16 = jnp.float32, jnp.float16, jnp.bfloat16
HIGH = lax.Precision.HIGH


def exponent(largest):
    return jnp.floor(jnp.log(jnp.clip(largest, 1e-30, 1e38)) * 1.4426950408889634)


def dot_t(a, b, **kw):
    return lax.dot_general(a, b, (((1,), (1,)), ((), ())), preferred_element_type=F32, **kw)


def passed(v, axis, by):
    n = lax.axis_size(axis)
    return lax.ppermute(v, axis, [(i, (i + by) % n) for i in range(n)])


def spread(v, axis):
    n = lax.axis_size(axis)
    return lax.all_to_all(jnp.broadcast_to(v[None], (n,) + v.shape), axis, 0, 0, tiled=True)


def halves(first, second):
    lane = lax.broadcasted_iota(jnp.int32, first.shape, 1)
    low = jnp.where(lane < 64, first, pltpu.roll(second, 64, 1))
    high = jnp.where(lane < 64, pltpu.roll(first, 64, 1), second)
    return low, high


def pack_kernel(cols, s_ref, a_ref, packed_ref):
    rows, ns = s_ref.shape
    nf = a_ref.shape[1]

    def put(at, value):
        top = value.astype(BF16)
        packed_ref[0, :, at : at + value.shape[1]] = top
        low = (value - top.astype(F32)).astype(BF16)
        packed_ref[1, :, at : at + value.shape[1]] = low

    total = jnp.zeros((rows, 128), F32)
    for at in range(0, ns, 128):
        value = s_ref[:, at : at + 128]
        total = total + jnp.abs(value)
        put(at, value)
    a_own = a_ref[...]
    bound_a = jnp.max(jnp.abs(a_own), axis=1, keepdims=True)
    bound = 0.125 * jnp.sum(total, axis=1, keepdims=True) + 0.75 * nf * bound_a
    lane = lax.broadcasted_iota(jnp.int32, (rows, nf), 1)
    exps = jnp.where(lane == 0, exponent(bound), exponent(0.125 * cols * bound_a)) + 2
    put(ns, jnp.concatenate([a_own, exps], axis=1))


def turn_kernel(nx, nz, parts_ref0, parts_ref1, out_ref):
    run = 128
    n = parts_ref0.shape[1]

    @pl.loop(0, nz)
    def _(z):
        for part, in_ref in enumerate((parts_ref0, parts_ref1)):
            for q in range(nx // 2):
                for k in range(nz // 2):
                    first = (q * nz + k) * run
                    second = first + nz // 2 * run
                    pair = halves(
                        in_ref[z, :, first : first + run].astype(F32),
                        in_ref[z, :, second : second + run].astype(F32),
                    )
                    for h, value in enumerate(pair):
                        at = ((2 * k + h) * nx // 2 + q) * run
                        out_ref[z, part * n : (part + 1) * n, at : at + run] = value.astype(BF16)


def cross_kernel(nx, nz, iz_ref, exps_ref, c0_ref, c1_ref, s_ref, place_ref, term_ref, out_ref):
    n, ns = c0_ref.shape[1:]
    cols, nf = s_ref.shape[0] // 2, place_ref.shape[2] // 2
    group = 128 // n
    pair = iz_ref[0] // 2
    scale = exps_ref[2], exps_ref[3]
    for part, c_ref in enumerate((c0_ref, c1_ref)):

        @pl.loop(0, nz // group)
        def _(step):
            zs = pl.ds(step * group, group)
            rows = c_ref[zs].reshape(group * n, ns)
            both = dot_t(rows, s_ref[...])
            term = term_ref[zs, part * n : (part + 1) * n, :].reshape(group * n, cols)
            cross = (both[:, :cols] + both[:, cols:] + term) * scale[0]
            share = jnp.zeros((group * n, 2 * nf), F32)
            for x in range(nx):
                at = pl.ds(pl.multiple_of(x * nz * 64 + pair * 128, 128), 128)
                picked = c_ref[zs, :, at].reshape(group * n, 128)
                share += jnp.dot(picked, place_ref[x], preferred_element_type=F32)
            share = (share[:, :nf] + share[:, nf:]) * scale[1]
            lane = lax.broadcasted_iota(jnp.int32, share.shape, 1)
            marks = jnp.where(lane == 0, exps_ref[0], exps_ref[1])
            tail = jnp.concatenate([share, marks], axis=1)
            here = pl.ds(part * n, n)
            out_ref[zs, here, :cols] = cross.reshape(group, n, cols)
            out_ref[zs, here, cols:] = tail.reshape(group, n, 2 * nf)


def diag_kernel(v_ref, c_ref, out_ref, parts_ref):
    nx, nz, rows, cols = v_ref.shape
    for z in range(nz):
        value = v_ref[:, z].reshape(nx * rows, cols)
        top = value.astype(BF16)
        parts_ref[0, :, z * cols : (z + 1) * cols] = top
        parts_ref[1, :, z * cols : (z + 1) * cols] = (value - top.astype(F32)).astype(BF16)

    @pl.loop(0, c_ref.shape[0] // 256)
    def _(step):
        at = pl.ds(pl.multiple_of(step * 256, 256), 256)
        c = c_ref[at, :]
        both = dot_t(parts_ref[0], c) + dot_t(parts_ref[1], c)
        out_ref[:, :, at] = both.reshape(nx, rows, 256)


def natural_kernel(nx, nz, in_ref, out_ref):
    rows = out_ref.shape[0]
    run = 2 * rows
    for q in range(nx // 2):
        for k in range(nz // 2):
            cut = slice(q * run, (q + 1) * run)
            pair = halves(in_ref[2 * k, :, cut], in_ref[2 * k + 1, :, cut])
            for h, value in enumerate(pair):
                at = ((2 * q + h) * nz // 2 + k) * run
                out_ref[:, at : at + run] = value


def shards(coupling, arrow_link, local_cov, boundary_cov, boundary_arrow, fixed_cov):
    c_own, link, local = coupling[0], arrow_link[0], local_cov[0]
    s_own, a_own = boundary_cov[0], boundary_arrow[0]
    nx, nz = lax.axis_size("x"), lax.axis_size("z")
    steps = lax.axis_size("y") * lax.axis_size("c")
    group = nx * nz
    rows, ns = c_own.shape
    nf = a_own.shape[1]
    cols = nx * rows
    ix, iz = lax.axis_index("x"), lax.axis_index("z")

    packed = pl.pallas_call(
        functools.partial(pack_kernel, cols),
        out_shape=jax.ShapeDtypeStruct((2, rows, ns + 2 * nf), BF16),
    )(s_own, a_own)
    route = [(t * group + b, (t - 1) * group + b) for t in range(1, steps) for b in range(group)]
    packed = lax.ppermute(packed, ("y", "c", "x", "z"), route)
    before, after = passed(packed, "x", 1), passed(packed, "x", -1)
    far_top, far_low = passed(packed[0], "x", 2), passed(packed[1], "x", -2)
    far = jnp.stack([far_top, far_low])
    s_cols = jnp.zeros((2, nx, rows, ns), BF16)
    tails = jnp.zeros((2, nx, rows, 2 * nf), BF16)
    for by, block in ((0, packed), (nx - 1, before), (1, after), (2, far)):
        at = (ix + by) % nx
        s_cols = lax.dynamic_update_index_in_dim(s_cols, block[..., :ns], at, 1)
        tails = lax.dynamic_update_index_in_dim(tails, block[..., ns:], at, 1)
    s_cols = s_cols.reshape(2 * cols, ns)
    a_two = tails[..., :nf].reshape(2, cols, nf)
    exps = jnp.max(tails[0, :, :, nf : nf + 2].astype(F32), axis=(0, 1))
    exps = jnp.concatenate([exps, jnp.exp2(14 - exps)])

    link_rows = lax.dynamic_slice_in_dim(link, ix * nz * rows, nz * rows, 0)
    term = dot_t(link_rows, a_two[0].astype(F32) + a_two[1].astype(F32), precision=HIGH)
    term = term.reshape(nz, rows, cols)
    place = jnp.concatenate([a_two[0], a_two[1]], axis=1).reshape(nx, 1, rows, 2 * nf)
    here = lax.broadcasted_iota(jnp.int32, (1, 2, 1, 1), 1) == iz % 2
    place = jnp.where(here, place, jnp.zeros((), BF16)).reshape(nx, 2 * rows, 2 * nf)

    half = rows // 2
    c_parts = spread(c_own[:half], "z"), lax.all_gather(c_own[half:], "z", axis=0)
    c_turned = pl.pallas_call(
        functools.partial(turn_kernel, nx, nz),
        out_shape=jax.ShapeDtypeStruct((nz, rows, ns), BF16),
        cost_estimate=pl.CostEstimate(flops=0, bytes_accessed=20 << 20, transcendentals=0),
        compiler_params=pltpu.CompilerParams(vmem_limit_bytes=16 << 20),
    )(*c_parts)
    in_smem, in_vmem = pl.BlockSpec(memory_space=pltpu.SMEM), pl.BlockSpec(memory_space=pltpu.VMEM)
    sent = pl.pallas_call(
        functools.partial(cross_kernel, nx, nz),
        out_shape=jax.ShapeDtypeStruct((nz, rows, cols + 2 * nf), F32),
        in_specs=[in_smem] * 2 + [in_vmem] * 5,
        compiler_params=pltpu.CompilerParams(vmem_limit_bytes=24 << 20),
    )(iz.reshape(1), exps, *c_parts, s_cols, place, term)
    sent = sent.astype(F16)
    sent = lax.all_to_all(sent, "z", 0, 0, tiled=True)
    cross = sent[..., :cols]
    marks = sent[:, :1, cols + nf : cols + nf + 2].astype(F32)
    scale = jnp.exp2(marks[..., :1] - 14)

    every = spread(cross, "x").astype(F32) * scale[None]
    diag = pl.pallas_call(
        diag_kernel,
        out_shape=jax.ShapeDtypeStruct((nx, rows, nz * rows), F32),
        scratch_shapes=[pltpu.VMEM((2, cols, ns), BF16)],
        compiler_params=pltpu.CompilerParams(vmem_limit_bytes=24 << 20),
    )(every, c_turned.reshape(nz * rows, ns))
    diag = lax.all_to_all(diag, "x", 0, 0, tiled=True)

    cross_rows = pl.pallas_call(
        functools.partial(natural_kernel, nx, nz),
        out_shape=jax.ShapeDtypeStruct((rows, ns), F32),
    )(cross.astype(F32) * scale)
    share = sent[..., cols : cols + nf].astype(F32) * jnp.exp2(marks[..., 1:] - 14)
    link_own = lax.dynamic_slice_in_dim(link, (ix * nz + iz) * rows, rows, 0)
    arrow = jnp.dot(link_own, fixed_cov, precision=lax.Precision.HIGHEST)
    arrow = jnp.sum(share, axis=0) + arrow
    local = lax.optimization_barrier(local + dot_t(arrow, link, precision=HIGH))
    diag_rows = local + diag.transpose(1, 0, 2).reshape(rows, ns)
    return (diag_rows[None], cross_rows[None], arrow[None])


def solution(mesh):
    mesh = Mesh(mesh.devices.reshape(8, 2, 4, 8), ("y", "c", "x", "z"))
    step, space = ("y", "c"), ("x", "z")
    row_split = P(step, space, None)
    return jax.shard_map(
        shards,
        mesh=mesh,
        in_specs=(row_split, P(step, None, None), row_split, row_split, row_split, P()),
        out_specs=(row_split, row_split, row_split),
        check_vma=False,
    )
```

```python
import functools

import jax
import jax.numpy as jnp
from jax import lax
from jax.experimental import pallas as pl
from jax.experimental.pallas import tpu as pltpu
from jax.sharding import Mesh, PartitionSpec as P

F32, F16, BF16 = jnp.float32, jnp.float16, jnp.bfloat16
HIGH = lax.Precision.HIGH


def exponent(largest):
    return jnp.floor(jnp.log(jnp.clip(largest, 1e-30, 1e38)) * 1.4426950408889634)


def dot_t(a, b, **kw):
    return lax.dot_general(a, b, (((1,), (1,)), ((), ())), preferred_element_type=F32, **kw)


def spread(v, axis):
    n = lax.axis_size(axis)
    return lax.all_to_all(jnp.broadcast_to(v[None], (n,) + v.shape), axis, 0, 0, tiled=True)


def halves(first, second):
    lane = lax.broadcasted_iota(jnp.int32, first.shape, 1)
    low = jnp.where(lane < 64, first, pltpu.roll(second, 64, 1))
    high = jnp.where(lane < 64, pltpu.roll(first, 64, 1), second)
    return low, high


def pack_kernel(cols, s_ref, a_ref, packed_ref):
    rows, ns = s_ref.shape
    nf = a_ref.shape[1]

    def put(at, value):
        top = value.astype(BF16)
        packed_ref[0, :, at : at + value.shape[1]] = top
        low = (value - top.astype(F32)).astype(BF16)
        packed_ref[1, :, at : at + value.shape[1]] = low

    total = jnp.zeros((rows, 128), F32)
    for at in range(0, ns, 128):
        value = s_ref[:, at : at + 128]
        total = total + jnp.abs(value)
        put(at, value)
    a_own = a_ref[...]
    bound_a = jnp.max(jnp.abs(a_own), axis=1, keepdims=True)
    bound = 0.125 * jnp.sum(total, axis=1, keepdims=True) + 0.75 * nf * bound_a
    lane = lax.broadcasted_iota(jnp.int32, (rows, nf), 1)
    exps = jnp.where(lane == 0, exponent(bound), exponent(0.125 * cols * bound_a)) + 2
    put(ns, jnp.concatenate([a_own, exps], axis=1))


def turn_kernel(nx, nz, in_ref, out_ref):
    run = 128

    @pl.loop(0, in_ref.shape[0] // 64)
    def _(step):
        at_rows = pl.ds(pl.multiple_of(step * 64, 64), 64)
        for q in range(nx // 2):
            for k in range(nz // 2):
                first = (q * nz + k) * run
                second = first + nz // 2 * run
                pair = halves(
                    in_ref[at_rows, first : first + run].astype(F32),
                    in_ref[at_rows, second : second + run].astype(F32),
                )
                for h, value in enumerate(pair):
                    at = ((2 * k + h) * nx // 2 + q) * run
                    out_ref[at_rows, at : at + run] = value.astype(BF16)


def cross_kernel(nz, iz_ref, exps_ref, c_ref, s_ref, place_ref, term_ref, out_ref):
    nx, _, rows, _ = s_ref.shape
    all_rows, ns = c_ref.shape
    nf = place_ref.shape[2] // 2
    run = 2 * rows
    lane = lax.broadcasted_iota(jnp.int32, (all_rows, run), 1)
    for q in range(nx // 2):
        block = s_ref[2 * q : 2 * q + 2, :, :, :ns].reshape(2 * run, ns)
        both = dot_t(c_ref[...], block)
        first, second = both[:, :run], both[:, run:]
        first = first + pltpu.roll(first, rows, 1)
        second = second + pltpu.roll(second, rows, 1)
        cross = jnp.where(lane < rows, first, second)
        at = slice(q * run, (q + 1) * run)
        out_ref[:, at] = (cross + term_ref[:, at]) * exps_ref[2]
    pair = iz_ref[0] // 2
    share = jnp.zeros((all_rows, 2 * nf), F32)
    for x in range(nx):
        at = pl.ds(pl.multiple_of(x * nz * rows + pair * run, run), run)
        share += jnp.dot(c_ref[:, at], place_ref[x], preferred_element_type=F32)
    share = (share + pltpu.roll(share, nf, 1)) * exps_ref[3]
    marks = jnp.where(lane == nf, exps_ref[0], exps_ref[1])
    out_ref[:, nx * rows :] = jnp.where(lane < nf, share, marks)


def diag_kernel(top_ref, low_ref, c_ref, out_ref, parts_ref):
    nx, nz, rows, cols = top_ref.shape
    for part, v_ref in enumerate((top_ref, low_ref)):
        for z in range(nz):
            value = v_ref[:, z].reshape(nx * rows, cols)
            parts_ref[part, :, z * cols : (z + 1) * cols] = value
    for at in range(0, c_ref.shape[0], 256):
        c = c_ref[at : at + 256, :]
        both = dot_t(parts_ref[0], c) + dot_t(parts_ref[1], c)
        out_ref[:, :, at : at + 256] = both.reshape(nx, rows, 256)


def natural_kernel(nx, nz, in_ref, out_ref):
    rows = out_ref.shape[0]
    run = 2 * rows
    for q in range(nx // 2):
        for k in range(nz // 2):
            cut = slice(q * run, (q + 1) * run)
            pair = halves(in_ref[2 * k, :, cut], in_ref[2 * k + 1, :, cut])
            for h, value in enumerate(pair):
                at = ((2 * q + h) * nz // 2 + k) * run
                out_ref[:, at : at + run] = value


def shards(coupling, arrow_link, local_cov, boundary_cov, boundary_arrow, fixed_cov):
    c_own, link, local = coupling[0], arrow_link[0], local_cov[0]
    s_own, a_own = boundary_cov[0], boundary_arrow[0]
    nx, nz = lax.axis_size("x"), lax.axis_size("z")
    steps = lax.axis_size("y") * lax.axis_size("c")
    group = nx * nz
    rows, ns = c_own.shape
    nf = a_own.shape[1]
    cols = nx * rows
    ix, iz = lax.axis_index("x"), lax.axis_index("z")

    packed = pl.pallas_call(
        functools.partial(pack_kernel, cols),
        out_shape=jax.ShapeDtypeStruct((2, rows, ns + 2 * nf), BF16),
    )(s_own, a_own)
    route = [(t * group + b, (t - 1) * group + b) for t in range(1, steps) for b in range(group)]
    packed = lax.ppermute(packed, ("y", "c", "x", "z"), route)
    succ = spread(packed, "x")
    tails = succ[..., ns:]
    a_two = tails[..., :nf]
    exps = jnp.max(tails[:, 0, :, nf : nf + 2].astype(F32), axis=(0, 1))
    exps = jnp.concatenate([exps, jnp.exp2(14 - exps)])

    link_rows = lax.dynamic_slice_in_dim(link, ix * nz * rows, nz * rows, 0)
    a_cols = a_two[:, 0].astype(F32) + a_two[:, 1].astype(F32)
    term = dot_t(link_rows, a_cols.reshape(cols, nf), precision=HIGH)
    place = jnp.concatenate([a_two[:, 0], a_two[:, 1]], axis=2)[:, None]
    here = lax.broadcasted_iota(jnp.int32, (1, 2, 1, 1), 1) == iz % 2
    place = jnp.where(here, place, jnp.zeros((), BF16)).reshape(nx, 2 * rows, 2 * nf)

    c_rows = lax.all_gather(c_own, "z", axis=0, tiled=True)
    c_turned = pl.pallas_call(
        functools.partial(turn_kernel, nx, nz),
        out_shape=jax.ShapeDtypeStruct(c_rows.shape, BF16),
        cost_estimate=pl.CostEstimate(flops=0, bytes_accessed=20 << 20, transcendentals=0),
        compiler_params=pltpu.CompilerParams(vmem_limit_bytes=16 << 20),
    )(c_rows)
    in_smem, in_vmem = pl.BlockSpec(memory_space=pltpu.SMEM), pl.BlockSpec(memory_space=pltpu.VMEM)
    sent = pl.pallas_call(
        functools.partial(cross_kernel, nz),
        out_shape=jax.ShapeDtypeStruct((nz * rows, cols + 2 * nf), F32),
        in_specs=[in_smem] * 2 + [in_vmem] * 4,
        compiler_params=pltpu.CompilerParams(vmem_limit_bytes=24 << 20),
    )(iz.reshape(1), exps, c_rows, succ, place, term)
    sent = sent.reshape(nz, rows, cols + 2 * nf)
    sent = sent.astype(F16)
    sent = lax.all_to_all(sent, "z", 0, 0, tiled=True)
    cross = sent[..., :cols]
    marks = sent[:, :1, cols + nf : cols + nf + 2].astype(F32)
    scale = jnp.exp2(marks[..., :1] - 14)

    every = spread(cross, "x").astype(F32) * scale[None]
    every_top = lax.reduce_precision(every, 8, 7)
    every_low = (every - every_top).astype(BF16)
    diag = pl.pallas_call(
        diag_kernel,
        out_shape=jax.ShapeDtypeStruct((nx, rows, nz * rows), F32),
        scratch_shapes=[pltpu.VMEM((2, cols, ns), BF16)],
        compiler_params=pltpu.CompilerParams(vmem_limit_bytes=24 << 20),
    )(every_top.astype(BF16), every_low, c_turned)
    diag = lax.all_to_all(diag, "x", 0, 0, tiled=True)

    cross_rows = pl.pallas_call(
        functools.partial(natural_kernel, nx, nz),
        out_shape=jax.ShapeDtypeStruct((rows, ns), F32),
    )(cross.astype(F32) * scale)
    share = sent[..., cols : cols + nf].astype(F32) * jnp.exp2(marks[..., 1:] - 14)
    link_own = lax.dynamic_slice_in_dim(link, (ix * nz + iz) * rows, rows, 0)
    arrow = jnp.dot(link_own, fixed_cov, precision=lax.Precision.HIGHEST)
    arrow = jnp.sum(share, axis=0) + arrow
    local = lax.optimization_barrier(local + dot_t(arrow, link, precision=HIGH))
    diag_rows = local + diag.transpose(1, 0, 2).reshape(rows, ns)
    return (diag_rows[None], cross_rows[None], arrow[None])


def solution(mesh):
    mesh = Mesh(mesh.devices.reshape(8, 2, 4, 8), ("y", "c", "x", "z"))
    step, space = ("y", "c"), ("x", "z")
    row_split = P(step, space, None)
    return jax.shard_map(
        shards,
        mesh=mesh,
        in_specs=(row_split, P(step, None, None), row_split, row_split, row_split, P()),
        out_specs=(row_split, row_split, row_split),
        check_vma=False,
    )
```

```python
import functools

import jax
import jax.numpy as jnp
from jax import lax
from jax.experimental import pallas as pl
from jax.experimental.pallas import tpu as pltpu
from jax.sharding import Mesh, PartitionSpec as P

F32, F16, BF16 = jnp.float32, jnp.float16, jnp.bfloat16
HIGH = lax.Precision.HIGH


def exponent(largest):
    return jnp.floor(jnp.log(jnp.clip(largest, 1e-30, 1e38)) * 1.4426950408889634)


def dot_t(a, b, **kw):
    return lax.dot_general(a, b, (((1,), (1,)), ((), ())), preferred_element_type=F32, **kw)


def passed(v, axis, by):
    n = lax.axis_size(axis)
    return lax.ppermute(v, axis, [(i, (i + by) % n) for i in range(n)])


def spread(v, axis):
    n = lax.axis_size(axis)
    return lax.all_to_all(jnp.broadcast_to(v[None], (n,) + v.shape), axis, 0, 0, tiled=True)


def halves(first, second):
    lane = lax.broadcasted_iota(jnp.int32, first.shape, 1)
    low = jnp.where(lane < 64, first, pltpu.roll(second, 64, 1))
    high = jnp.where(lane < 64, pltpu.roll(first, 64, 1), second)
    return low, high


def pack_kernel(cols, s_ref, a_ref, packed_ref):
    rows, ns = s_ref.shape
    nf = a_ref.shape[1]

    def put(at, value):
        top = value.astype(BF16)
        packed_ref[0, :, at : at + value.shape[1]] = top
        low = (value - top.astype(F32)).astype(BF16)
        packed_ref[1, :, at : at + value.shape[1]] = low

    total = jnp.zeros((rows, 128), F32)
    for at in range(0, ns, 128):
        value = s_ref[:, at : at + 128]
        total = total + jnp.abs(value)
        put(at, value)
    a_own = a_ref[...]
    bound_a = jnp.max(jnp.abs(a_own), axis=1, keepdims=True)
    bound = 0.125 * jnp.sum(total, axis=1, keepdims=True) + 0.75 * nf * bound_a
    lane = lax.broadcasted_iota(jnp.int32, (rows, nf), 1)
    exps = jnp.where(lane == 0, exponent(bound), exponent(0.125 * cols * bound_a)) + 2
    put(ns, jnp.concatenate([a_own, exps], axis=1))


def turn_kernel(nx, nz, in_ref, out_ref):
    run = 128

    @pl.loop(0, in_ref.shape[0] // 64)
    def _(step):
        at_rows = pl.ds(pl.multiple_of(step * 64, 64), 64)
        for q in range(nx // 2):
            for k in range(nz // 2):
                first = (q * nz + k) * run
                second = first + nz // 2 * run
                pair = halves(
                    in_ref[at_rows, first : first + run].astype(F32),
                    in_ref[at_rows, second : second + run].astype(F32),
                )
                for h, value in enumerate(pair):
                    at = ((2 * k + h) * nx // 2 + q) * run
                    out_ref[at_rows, at : at + run] = value.astype(BF16)


def place_kernel(iz_ref, tails_ref, out_ref):
    rows, run = tails_ref.shape[2:]
    lane = lax.broadcasted_iota(jnp.int32, (rows, run), 1)
    odd = lax.rem(iz_ref[0], 2)
    for x in range(tails_ref.shape[0]):
        top = tails_ref[x, 0].astype(F32)
        low = pltpu.roll(tails_ref[x, 1].astype(F32), run // 2, 1)
        both = jnp.where(lane < run // 2, top, low)
        out_ref[x, :rows] = jnp.where(odd == 0, both, 0.0).astype(BF16)
        out_ref[x, rows:] = jnp.where(odd == 1, both, 0.0).astype(BF16)


def cross_kernel(order, iz_ref, exps_ref, s_ref, place_ref, term_ref, *refs):
    block_refs, (out_ref, c_ref) = refs[:-2], refs[-2:]
    nx, _, rows, _ = s_ref.shape
    nz = len(order)
    for by, block_ref in zip(order, block_refs):
        at = lax.rem(iz_ref[0] + by + nz, nz) * rows
        c_ref[pl.ds(pl.multiple_of(at, rows), rows), :] = block_ref[...]
    all_rows, ns = c_ref.shape
    nf = place_ref.shape[2] // 2
    run = 2 * rows
    lane = lax.broadcasted_iota(jnp.int32, (all_rows, run), 1)
    for q in range(nx // 2):
        block = s_ref[2 * q : 2 * q + 2, :, :, :ns].reshape(2 * run, ns)
        both = dot_t(c_ref[...], block)
        first, second = both[:, :run], both[:, run:]
        first = first + pltpu.roll(first, rows, 1)
        second = second + pltpu.roll(second, rows, 1)
        cross = jnp.where(lane < rows, first, second)
        at = slice(q * run, (q + 1) * run)
        out_ref[:, at] = (cross + term_ref[:, at]) * exps_ref[2]
    pair = iz_ref[0] // 2
    share = jnp.zeros((all_rows, 2 * nf), F32)
    for x in range(nx):
        at = pl.ds(pl.multiple_of(x * nz * rows + pair * run, run), run)
        share += jnp.dot(c_ref[:, at], place_ref[x], preferred_element_type=F32)
    share = (share + pltpu.roll(share, nf, 1)) * exps_ref[3]
    marks = jnp.where(lane == nf, exps_ref[0], exps_ref[1])
    out_ref[:, nx * rows :] = jnp.where(lane < nf, share, marks)


def diag_kernel(top_ref, low_ref, c_ref, out_ref, parts_ref):
    nx, nz, rows, cols = top_ref.shape
    for part, v_ref in enumerate((top_ref, low_ref)):
        for z in range(nz):
            value = v_ref[:, z].reshape(nx * rows, cols)
            parts_ref[part, :, z * cols : (z + 1) * cols] = value
    for at in range(0, c_ref.shape[0], 256):
        c = c_ref[at : at + 256, :]
        both = dot_t(parts_ref[0], c) + dot_t(parts_ref[1], c)
        out_ref[:, :, at : at + 256] = both.reshape(nx, rows, 256)


def natural_kernel(nx, nz, in_ref, out_ref):
    rows = out_ref.shape[0]
    run = 2 * rows
    for q in range(nx // 2):
        for k in range(nz // 2):
            cut = slice(q * run, (q + 1) * run)
            pair = halves(in_ref[2 * k, :, cut], in_ref[2 * k + 1, :, cut])
            for h, value in enumerate(pair):
                at = ((2 * q + h) * nz // 2 + k) * run
                out_ref[:, at : at + run] = value


def shards(coupling, arrow_link, local_cov, boundary_cov, boundary_arrow, fixed_cov):
    c_own, link, local = coupling[0], arrow_link[0], local_cov[0]
    s_own, a_own = boundary_cov[0], boundary_arrow[0]
    nx, nz = lax.axis_size("x"), lax.axis_size("z")
    steps = lax.axis_size("y") * lax.axis_size("c")
    group = nx * nz
    rows, ns = c_own.shape
    nf = a_own.shape[1]
    cols = nx * rows
    ix, iz = lax.axis_index("x"), lax.axis_index("z")

    packed = pl.pallas_call(
        functools.partial(pack_kernel, cols),
        out_shape=jax.ShapeDtypeStruct((2, rows, ns + 2 * nf), BF16),
    )(s_own, a_own)
    route = [(t * group + b, (t - 1) * group + b) for t in range(1, steps) for b in range(group)]
    packed = lax.ppermute(packed, ("y", "c", "x", "z"), route)
    succ = spread(packed, "x")
    tails = succ[..., ns:]
    a_two = tails[..., :nf]
    exps = jnp.max(tails[:, 0, :, nf : nf + 2].astype(F32), axis=(0, 1))
    exps = jnp.concatenate([exps, jnp.exp2(14 - exps)])

    link_rows = lax.dynamic_slice_in_dim(link, ix * nz * rows, nz * rows, 0)
    a_cols = a_two[:, 0].astype(F32) + a_two[:, 1].astype(F32)
    term = dot_t(link_rows, a_cols.reshape(cols, nf), precision=HIGH)
    in_smem, in_vmem = pl.BlockSpec(memory_space=pltpu.SMEM), pl.BlockSpec(memory_space=pltpu.VMEM)
    place = pl.pallas_call(
        place_kernel,
        out_shape=jax.ShapeDtypeStruct((nx, 2 * rows, 2 * nf), BF16),
        in_specs=[in_smem, in_vmem],
        cost_estimate=pl.CostEstimate(flops=10**11, bytes_accessed=1 << 20, transcendentals=0),
    )(iz.reshape(1), tails)

    c_blocks = [c_own] + [passed(c_own, "z", -by) for by in (1, -1, 2, -2, 4)]
    c_blocks += [passed(c_blocks[3], "z", -1), passed(c_blocks[4], "z", 1)]
    sent, c_rows = pl.pallas_call(
        functools.partial(cross_kernel, (0, 1, -1, 2, -2, 4, 3, -3)),
        out_shape=(
            jax.ShapeDtypeStruct((nz * rows, cols + 2 * nf), F32),
            jax.ShapeDtypeStruct((nz * rows, ns), BF16),
        ),
        in_specs=[in_smem] * 2 + [in_vmem] * (3 + len(c_blocks)),
        compiler_params=pltpu.CompilerParams(vmem_limit_bytes=16 << 20),
    )(iz.reshape(1), exps, succ, place, term, *c_blocks)
    c_turned = pl.pallas_call(
        functools.partial(turn_kernel, nx, nz),
        out_shape=jax.ShapeDtypeStruct(c_rows.shape, BF16),
        cost_estimate=pl.CostEstimate(flops=0, bytes_accessed=20 << 20, transcendentals=0),
        compiler_params=pltpu.CompilerParams(vmem_limit_bytes=8 << 20),
    )(c_rows)
    sent = sent.reshape(nz, rows, cols + 2 * nf)
    sent = sent.astype(F16)
    sent = lax.all_to_all(sent, "z", 0, 0, tiled=True)
    cross = sent[..., :cols]
    marks = sent[:, :1, cols + nf : cols + nf + 2].astype(F32)
    scale = jnp.exp2(marks[..., :1] - 14)

    every = spread(cross, "x").astype(F32) * scale[None]
    every_top = lax.reduce_precision(every, 8, 7)
    every_low = (every - every_top).astype(BF16)
    diag = pl.pallas_call(
        diag_kernel,
        out_shape=jax.ShapeDtypeStruct((nx, rows, nz * rows), F32),
        scratch_shapes=[pltpu.VMEM((2, cols, ns), BF16)],
        compiler_params=pltpu.CompilerParams(vmem_limit_bytes=12 << 20),
    )(every_top.astype(BF16), every_low, c_turned)
    diag = lax.all_to_all(diag, "x", 0, 0, tiled=True)

    cross_rows = pl.pallas_call(
        functools.partial(natural_kernel, nx, nz),
        out_shape=jax.ShapeDtypeStruct((rows, ns), F32),
    )(cross.astype(F32) * scale)
    share = sent[..., cols : cols + nf].astype(F32) * jnp.exp2(marks[..., 1:] - 14)
    link_own = lax.dynamic_slice_in_dim(link, (ix * nz + iz) * rows, rows, 0)
    arrow = jnp.dot(link_own, fixed_cov, precision=lax.Precision.HIGHEST)
    arrow = jnp.sum(share, axis=0) + arrow
    local = lax.optimization_barrier(local + dot_t(arrow, link, precision=HIGH))
    diag_rows = local + diag.transpose(1, 0, 2).reshape(rows, ns)
    return (diag_rows[None], cross_rows[None], arrow[None])


def solution(mesh):
    mesh = Mesh(mesh.devices.reshape(8, 2, 4, 8), ("y", "c", "x", "z"))
    step, space = ("y", "c"), ("x", "z")
    row_split = P(step, space, None)
    return jax.shard_map(
        shards,
        mesh=mesh,
        in_specs=(row_split, P(step, None, None), row_split, row_split, row_split, P()),
        out_specs=(row_split, row_split, row_split),
        check_vma=False,
    )
```

```python
import functools

import jax
import jax.numpy as jnp
from jax import lax
from jax.experimental import pallas as pl
from jax.experimental.pallas import tpu as pltpu
from jax.sharding import Mesh, PartitionSpec as P

F32, F16, BF16 = jnp.float32, jnp.float16, jnp.bfloat16
HIGH = lax.Precision.HIGH


def exponent(largest):
    return jnp.floor(jnp.log(jnp.clip(largest, 1e-30, 1e38)) * 1.4426950408889634)


def dot_t(a, b, **kw):
    return lax.dot_general(a, b, (((1,), (1,)), ((), ())), preferred_element_type=F32, **kw)


def spread(v, axis):
    n = lax.axis_size(axis)
    return lax.all_to_all(jnp.broadcast_to(v[None], (n,) + v.shape), axis, 0, 0, tiled=True)


def halves(first, second):
    lane = lax.broadcasted_iota(jnp.int32, first.shape, 1)
    low = jnp.where(lane < 64, first, pltpu.roll(second, 64, 1))
    high = jnp.where(lane < 64, pltpu.roll(first, 64, 1), second)
    return low, high


def pack_kernel(cols, s_ref, a_ref, packed_ref):
    rows, ns = s_ref.shape
    nf = a_ref.shape[1]

    def put(at, value):
        top = value.astype(BF16)
        packed_ref[0, :, at : at + value.shape[1]] = top
        low = (value - top.astype(F32)).astype(BF16)
        packed_ref[1, :, at : at + value.shape[1]] = low

    total = jnp.zeros((rows, 128), F32)
    for at in range(0, ns, 128):
        value = s_ref[:, at : at + 128]
        total = total + jnp.abs(value)
        put(at, value)
    a_own = a_ref[...]
    bound_a = jnp.max(jnp.abs(a_own), axis=1, keepdims=True)
    bound = 0.125 * jnp.sum(total, axis=1, keepdims=True) + 0.75 * nf * bound_a
    lane = lax.broadcasted_iota(jnp.int32, (rows, nf), 1)
    exps = jnp.where(lane == 0, exponent(bound), exponent(0.125 * cols * bound_a)) + 2
    put(ns, jnp.concatenate([a_own, exps], axis=1))


def turn_kernel(nx, nz, in_ref, out_ref):
    run = 128

    @pl.loop(0, in_ref.shape[0] // 64)
    def _(step):
        at_rows = pl.ds(pl.multiple_of(step * 64, 64), 64)
        for q in range(nx // 2):
            for k in range(nz // 2):
                first = (q * nz + k) * run
                second = first + nz // 2 * run
                pair = halves(
                    in_ref[at_rows, first : first + run].astype(F32),
                    in_ref[at_rows, second : second + run].astype(F32),
                )
                for h, value in enumerate(pair):
                    at = ((2 * k + h) * nx // 2 + q) * run
                    out_ref[at_rows, at : at + run] = value.astype(BF16)


def place_kernel(iz_ref, tails_ref, out_ref):
    rows, run = tails_ref.shape[2:]
    lane = lax.broadcasted_iota(jnp.int32, (rows, run), 1)
    odd = lax.rem(iz_ref[0], 2)
    for x in range(tails_ref.shape[0]):
        top = tails_ref[x, 0].astype(F32)
        low = pltpu.roll(tails_ref[x, 1].astype(F32), run // 2, 1)
        both = jnp.where(lane < run // 2, top, low)
        out_ref[x, :rows] = jnp.where(odd == 0, both, 0.0).astype(BF16)
        out_ref[x, rows:] = jnp.where(odd == 1, both, 0.0).astype(BF16)


def cross_kernel(nz, iz_ref, exps_ref, c_ref, s_ref, place_ref, term_ref, out_ref):
    nx, _, rows, _ = s_ref.shape
    all_rows, ns = c_ref.shape
    nf = place_ref.shape[2] // 2
    run = 2 * rows
    lane = lax.broadcasted_iota(jnp.int32, (all_rows, run), 1)
    for q in range(nx // 2):
        block = s_ref[2 * q : 2 * q + 2, :, :, :ns].reshape(2 * run, ns)
        both = dot_t(c_ref[...], block)
        first, second = both[:, :run], both[:, run:]
        first = first + pltpu.roll(first, rows, 1)
        second = second + pltpu.roll(second, rows, 1)
        cross = jnp.where(lane < rows, first, second)
        at = slice(q * run, (q + 1) * run)
        out_ref[:, at] = (cross + term_ref[:, at]) * exps_ref[2]
    pair = iz_ref[0] // 2
    share = jnp.zeros((all_rows, 2 * nf), F32)
    for x in range(nx):
        at = pl.ds(pl.multiple_of(x * nz * rows + pair * run, run), run)
        share += jnp.dot(c_ref[:, at], place_ref[x], preferred_element_type=F32)
    share = (share + pltpu.roll(share, nf, 1)) * exps_ref[3]
    marks = jnp.where(lane == nf, exps_ref[0], exps_ref[1])
    out_ref[:, nx * rows :] = jnp.where(lane < nf, share, marks)


def diag_kernel(top_ref, low_ref, c_ref, out_ref, parts_ref):
    nx, nz, rows, cols = top_ref.shape
    for part, v_ref in enumerate((top_ref, low_ref)):
        for z in range(nz):
            value = v_ref[:, z].reshape(nx * rows, cols)
            parts_ref[part, :, z * cols : (z + 1) * cols] = value
    for at in range(0, c_ref.shape[0], 256):
        c = c_ref[at : at + 256, :]
        both = dot_t(parts_ref[0], c) + dot_t(parts_ref[1], c)
        out_ref[:, :, at : at + 256] = both.reshape(nx, rows, 256)


def natural_kernel(nx, nz, in_ref, out_ref):
    rows = out_ref.shape[0]
    run = 2 * rows
    for q in range(nx // 2):
        for k in range(nz // 2):
            cut = slice(q * run, (q + 1) * run)
            pair = halves(in_ref[2 * k, :, cut], in_ref[2 * k + 1, :, cut])
            for h, value in enumerate(pair):
                at = ((2 * q + h) * nz // 2 + k) * run
                out_ref[:, at : at + run] = value


def shards(coupling, arrow_link, local_cov, boundary_cov, boundary_arrow, fixed_cov):
    c_own, link, local = coupling[0], arrow_link[0], local_cov[0]
    s_own, a_own = boundary_cov[0], boundary_arrow[0]
    nx, nz = lax.axis_size("x"), lax.axis_size("z")
    steps = lax.axis_size("y") * lax.axis_size("c")
    group = nx * nz
    rows, ns = c_own.shape
    nf = a_own.shape[1]
    cols = nx * rows
    ix, iz = lax.axis_index("x"), lax.axis_index("z")

    route = [(t * group + b, (t - 1) * group + b) for t in range(1, steps) for b in range(group)]
    s_own, a_own = lax.ppermute((s_own, a_own), ("y", "c", "x", "z"), route)
    packed = pl.pallas_call(
        functools.partial(pack_kernel, cols),
        out_shape=jax.ShapeDtypeStruct((2, rows, ns + 2 * nf), BF16),
    )(s_own, a_own)
    succ = jnp.zeros((nx,) + packed.shape, BF16)
    for by in range(nx):
        block = lax.ppermute(packed, "x", [((i + by) % nx, i) for i in range(nx)]) if by else packed
        succ = lax.dynamic_update_index_in_dim(succ, block, (ix + by) % nx, 0)
    tails = succ[..., ns:]
    a_two = tails[..., :nf]
    exps = jnp.max(tails[:, 0, :, nf : nf + 2].astype(F32), axis=(0, 1))
    exps = jnp.concatenate([exps, jnp.exp2(14 - exps)])

    link_rows = lax.dynamic_slice_in_dim(link, ix * nz * rows, nz * rows, 0)
    a_cols = a_two[:, 0].astype(F32) + a_two[:, 1].astype(F32)
    term = dot_t(link_rows, a_cols.reshape(cols, nf), precision=HIGH)
    in_smem, in_vmem = pl.BlockSpec(memory_space=pltpu.SMEM), pl.BlockSpec(memory_space=pltpu.VMEM)
    place = pl.pallas_call(
        place_kernel,
        out_shape=jax.ShapeDtypeStruct((nx, 2 * rows, 2 * nf), BF16),
        in_specs=[in_smem, in_vmem],
    )(iz.reshape(1), tails)

    c_rows = spread(c_own, "z").reshape(nz * rows, ns)
    sent = pl.pallas_call(
        functools.partial(cross_kernel, nz),
        out_shape=jax.ShapeDtypeStruct((nz * rows, cols + 2 * nf), F32),
        in_specs=[in_smem] * 2 + [in_vmem] * 4,
        compiler_params=pltpu.CompilerParams(vmem_limit_bytes=12 << 20),
    )(iz.reshape(1), exps, c_rows, succ, place, term)
    c_turned = pl.pallas_call(
        functools.partial(turn_kernel, nx, nz),
        out_shape=jax.ShapeDtypeStruct(c_rows.shape, BF16),
        cost_estimate=pl.CostEstimate(flops=0, bytes_accessed=20 << 20, transcendentals=0),
        compiler_params=pltpu.CompilerParams(vmem_limit_bytes=8 << 20),
    )(c_rows)
    sent = sent.reshape(nz, rows, cols + 2 * nf)
    sent = sent.astype(F16)
    sent = lax.all_to_all(sent, "z", 0, 0, tiled=True)
    cross = sent[..., :cols]
    marks = sent[:, :1, cols + nf : cols + nf + 2].astype(F32)
    scale = jnp.exp2(marks[..., :1] - 14)

    every = spread(cross, "x").astype(F32) * scale[None]
    every_top = lax.reduce_precision(every, 8, 7)
    every_low = (every - every_top).astype(BF16)
    diag = pl.pallas_call(
        diag_kernel,
        out_shape=jax.ShapeDtypeStruct((nx, rows, nz * rows), F32),
        scratch_shapes=[pltpu.VMEM((2, cols, ns), BF16)],
        compiler_params=pltpu.CompilerParams(vmem_limit_bytes=12 << 20),
    )(every_top.astype(BF16), every_low, c_turned)
    diag = lax.all_to_all(diag, "x", 0, 0, tiled=True)

    cross_rows = pl.pallas_call(
        functools.partial(natural_kernel, nx, nz),
        out_shape=jax.ShapeDtypeStruct((rows, ns), F32),
    )(cross.astype(F32) * scale)
    share = sent[..., cols : cols + nf].astype(F32) * jnp.exp2(marks[..., 1:] - 14)
    link_own = lax.dynamic_slice_in_dim(link, (ix * nz + iz) * rows, rows, 0)
    arrow = jnp.dot(link_own, fixed_cov, precision=lax.Precision.HIGHEST)
    arrow = jnp.sum(share, axis=0) + arrow
    local = lax.optimization_barrier(local + dot_t(arrow, link, precision=HIGH))
    diag_rows = local + diag.transpose(1, 0, 2).reshape(rows, ns)
    return (diag_rows[None], cross_rows[None], arrow[None])


def solution(mesh):
    mesh = Mesh(mesh.devices.reshape(8, 2, 4, 8), ("y", "c", "x", "z"))
    step, space = ("y", "c"), ("x", "z")
    row_split = P(step, space, None)
    return jax.shard_map(
        shards,
        mesh=mesh,
        in_specs=(row_split, P(step, None, None), row_split, row_split, row_split, P()),
        out_specs=(row_split, row_split, row_split),
        check_vma=False,
    )
```

```python
import functools

import jax
import jax.numpy as jnp
from jax import lax
from jax.experimental import pallas as pl
from jax.experimental.pallas import tpu as pltpu
from jax.sharding import Mesh, PartitionSpec as P

F32, F16, BF16 = jnp.float32, jnp.float16, jnp.bfloat16
HIGH = lax.Precision.HIGH


def exponent(largest):
    return jnp.floor(jnp.log(jnp.clip(largest, 1e-30, 1e38)) * 1.4426950408889634)


def dot_t(a, b, **kw):
    return lax.dot_general(a, b, (((1,), (1,)), ((), ())), preferred_element_type=F32, **kw)


def spread(v, axis):
    n = lax.axis_size(axis)
    return lax.all_to_all(jnp.broadcast_to(v[None], (n,) + v.shape), axis, 0, 0, tiled=True)


def halves(first, second):
    lane = lax.broadcasted_iota(jnp.int32, first.shape, 1)
    low = jnp.where(lane < 64, first, pltpu.roll(second, 64, 1))
    high = jnp.where(lane < 64, pltpu.roll(first, 64, 1), second)
    return low, high


def pack_kernel(s_ref, a_ref, packed_ref):
    rows, ns = s_ref.shape
    nf = a_ref.shape[1]

    def put(at, value):
        top = value.astype(BF16)
        packed_ref[0, :, at : at + value.shape[1]] = top
        low = (value - top.astype(F32)).astype(BF16)
        packed_ref[1, :, at : at + value.shape[1]] = low

    total = jnp.zeros((rows, 128), F32)
    for at in range(0, ns, 128):
        value = s_ref[:, at : at + 128]
        total = total + jnp.abs(value)
        put(at, value)
    a_own = a_ref[...]
    bound_a = jnp.max(jnp.abs(a_own), axis=1, keepdims=True)
    bound = 0.125 * jnp.sum(total, axis=1, keepdims=True) + 0.75 * nf * bound_a
    exps = jnp.broadcast_to(exponent(bound) + 2, a_own.shape)
    put(ns, jnp.concatenate([a_own, exps], axis=1))


def turn_kernel(nx, nz, in_ref, out_ref):
    run = 128

    @pl.loop(0, in_ref.shape[0] // 64)
    def _(step):
        at_rows = pl.ds(pl.multiple_of(step * 64, 64), 64)
        for q in range(nx // 2):
            for k in range(nz // 2):
                first = (q * nz + k) * run
                second = first + nz // 2 * run
                pair = halves(
                    in_ref[at_rows, first : first + run].astype(F32),
                    in_ref[at_rows, second : second + run].astype(F32),
                )
                for h, value in enumerate(pair):
                    at = ((2 * k + h) * nx // 2 + q) * run
                    out_ref[at_rows, at : at + run] = value.astype(BF16)


def place_kernel(iz_ref, tails_ref, out_ref):
    rows, run = tails_ref.shape[2:]
    lane = lax.broadcasted_iota(jnp.int32, (rows, run), 1)
    odd = lax.rem(iz_ref[0], 2)
    for x in range(tails_ref.shape[0]):
        top = tails_ref[x, 0].astype(F32)
        low = pltpu.roll(tails_ref[x, 1].astype(F32), run // 2, 1)
        both = jnp.where(lane < run // 2, top, low)
        out_ref[x, :rows] = jnp.where(odd == 0, both, 0.0).astype(BF16)
        out_ref[x, rows:] = jnp.where(odd == 1, both, 0.0).astype(BF16)


def cross_kernel(nz, iz_ref, exps_ref, c_ref, s_ref, place_ref, term_ref, out_ref, share_ref):
    nx, _, rows, _ = s_ref.shape
    all_rows, ns = c_ref.shape
    nf = place_ref.shape[2] // 2
    run = 2 * rows
    lane = lax.broadcasted_iota(jnp.int32, (all_rows, run), 1)
    for q in range(nx // 2):
        block = s_ref[2 * q : 2 * q + 2, :, :, :ns].reshape(2 * run, ns)
        both = dot_t(c_ref[...], block)
        first, second = both[:, :run], both[:, run:]
        first = first + pltpu.roll(first, rows, 1)
        second = second + pltpu.roll(second, rows, 1)
        cross = jnp.where(lane < rows, first, second)
        at = slice(q * run, (q + 1) * run)
        out_ref[:, at] = (cross + term_ref[:, at]) * exps_ref[1]
    pair = iz_ref[0] // 2
    share = jnp.zeros((all_rows, 2 * nf), F32)
    for x in range(nx):
        at = pl.ds(pl.multiple_of(x * nz * rows + pair * run, run), run)
        share += jnp.dot(c_ref[:, at], place_ref[x], preferred_element_type=F32)
    share = share + pltpu.roll(share, nf, 1)
    share_ref[...] = jnp.where(lane < nf, share, exps_ref[0])


def diag_kernel(top_ref, low_ref, c_ref, out_ref, parts_ref):
    nx, nz, rows, cols = top_ref.shape
    for part, v_ref in enumerate((top_ref, low_ref)):
        for z in range(nz):
            value = v_ref[:, z].reshape(nx * rows, cols)
            parts_ref[part, :, z * cols : (z + 1) * cols] = value
    for at in range(0, c_ref.shape[0], 256):
        c = c_ref[at : at + 256, :]
        both = dot_t(parts_ref[0], c) + dot_t(parts_ref[1], c)
        out_ref[:, :, at : at + 256] = both.reshape(nx, rows, 256)


def natural_kernel(nx, nz, in_ref, out_ref):
    rows = out_ref.shape[0]
    run = 2 * rows
    for q in range(nx // 2):
        for k in range(nz // 2):
            cut = slice(q * run, (q + 1) * run)
            pair = halves(in_ref[2 * k, :, cut], in_ref[2 * k + 1, :, cut])
            for h, value in enumerate(pair):
                at = ((2 * q + h) * nz // 2 + k) * run
                out_ref[:, at : at + run] = value


def shards(coupling, arrow_link, local_cov, boundary_cov, boundary_arrow, fixed_cov):
    c_own, link, local = coupling[0], arrow_link[0], local_cov[0]
    s_own, a_own = boundary_cov[0], boundary_arrow[0]
    nx, nz = lax.axis_size("x"), lax.axis_size("z")
    steps = lax.axis_size("y") * lax.axis_size("c")
    group = nx * nz
    rows, ns = c_own.shape
    nf = a_own.shape[1]
    cols = nx * rows
    ix, iz = lax.axis_index("x"), lax.axis_index("z")

    route = [(t * group + b, (t - 1) * group + b) for t in range(1, steps) for b in range(group)]
    s_own, a_own = lax.ppermute((s_own, a_own), ("y", "c", "x", "z"), route)
    packed = pl.pallas_call(
        pack_kernel,
        out_shape=jax.ShapeDtypeStruct((2, rows, ns + 2 * nf), BF16),
    )(s_own, a_own)
    succ = jnp.zeros((nx,) + packed.shape, BF16)
    for by in range(nx):
        block = lax.ppermute(packed, "x", [((i + by) % nx, i) for i in range(nx)]) if by else packed
        succ = lax.dynamic_update_index_in_dim(succ, block, (ix + by) % nx, 0)
    tails = succ[..., ns:]
    a_two = tails[..., :nf]
    exp_own = jnp.max(tails[:, 0, :, nf].astype(F32))
    exps = jnp.stack([exp_own, jnp.exp2(14 - exp_own)])

    link_rows = lax.dynamic_slice_in_dim(link, ix * nz * rows, nz * rows, 0)
    a_cols = a_two[:, 0].astype(F32) + a_two[:, 1].astype(F32)
    term = dot_t(link_rows, a_cols.reshape(cols, nf), precision=HIGH)
    in_smem, in_vmem = pl.BlockSpec(memory_space=pltpu.SMEM), pl.BlockSpec(memory_space=pltpu.VMEM)
    place = pl.pallas_call(
        place_kernel,
        out_shape=jax.ShapeDtypeStruct((nx, 2 * rows, 2 * nf), BF16),
        in_specs=[in_smem, in_vmem],
    )(iz.reshape(1), tails)

    c_rows = spread(c_own, "z").reshape(nz * rows, ns)
    sent, share = pl.pallas_call(
        functools.partial(cross_kernel, nz),
        out_shape=(
            jax.ShapeDtypeStruct((nz * rows, cols), F32),
            jax.ShapeDtypeStruct((nz * rows, 2 * nf), F32),
        ),
        in_specs=[in_smem] * 2 + [in_vmem] * 4,
        compiler_params=pltpu.CompilerParams(vmem_limit_bytes=12 << 20),
    )(iz.reshape(1), exps, c_rows, succ, place, term)
    c_turned = pl.pallas_call(
        functools.partial(turn_kernel, nx, nz),
        out_shape=jax.ShapeDtypeStruct(c_rows.shape, BF16),
        cost_estimate=pl.CostEstimate(flops=0, bytes_accessed=20 << 20, transcendentals=0),
        compiler_params=pltpu.CompilerParams(vmem_limit_bytes=8 << 20),
    )(c_rows)
    sent = sent.astype(F16).reshape(nz, rows, cols)
    sent = jnp.broadcast_to(sent[None], (nx, nz, rows, cols)).reshape(group, rows, cols)
    every = lax.all_to_all(sent, ("x", "z"), 0, 0, tiled=True).reshape(nx, nz, rows, cols)

    share = share.reshape(nz, rows, 2 * nf)
    arrow = jnp.zeros((rows, nf), F32)
    exp_z = jnp.zeros((nz,), F32)
    for by in range(nz):
        part = lax.dynamic_index_in_dim(share, (iz + by) % nz, 0, keepdims=False)
        part = lax.ppermute(part, "z", [(i, (i + by) % nz) for i in range(nz)]) if by else part
        arrow = arrow + part[:, :nf]
        exp_z = jnp.where(jnp.arange(nz) == (iz - by) % nz, part[0, nf], exp_z)
    scale = jnp.exp2(exp_z - 14)[:, None, None]
    cross = lax.dynamic_index_in_dim(every, ix, 0, keepdims=False)

    every = every.astype(F32) * scale[None]
    every_top = lax.reduce_precision(every, 8, 7)
    every_low = (every - every_top).astype(BF16)
    diag = pl.pallas_call(
        diag_kernel,
        out_shape=jax.ShapeDtypeStruct((nx, rows, nz * rows), F32),
        scratch_shapes=[pltpu.VMEM((2, cols, ns), BF16)],
        compiler_params=pltpu.CompilerParams(vmem_limit_bytes=12 << 20),
    )(every_top.astype(BF16), every_low, c_turned)
    diag = lax.all_to_all(diag, "x", 0, 0, tiled=True)

    cross_rows = pl.pallas_call(
        functools.partial(natural_kernel, nx, nz),
        out_shape=jax.ShapeDtypeStruct((rows, ns), F32),
    )(cross.astype(F32) * scale)
    link_own = lax.dynamic_slice_in_dim(link, (ix * nz + iz) * rows, rows, 0)
    arrow = arrow + jnp.dot(link_own, fixed_cov, precision=lax.Precision.HIGHEST)
    local = lax.optimization_barrier(local + dot_t(arrow, link, precision=HIGH))
    diag_rows = local + diag.transpose(1, 0, 2).reshape(rows, ns)
    return (diag_rows[None], cross_rows[None], arrow[None])


def solution(mesh):
    mesh = Mesh(mesh.devices.reshape(8, 2, 4, 8), ("y", "c", "x", "z"))
    step, space = ("y", "c"), ("x", "z")
    row_split = P(step, space, None)
    return jax.shard_map(
        shards,
        mesh=mesh,
        in_specs=(row_split, P(step, None, None), row_split, row_split, row_split, P()),
        out_specs=(row_split, row_split, row_split),
        check_vma=False,
    )
```

```python
import functools

import jax
import jax.numpy as jnp
from jax import lax
from jax.experimental import pallas as pl
from jax.experimental.pallas import tpu as pltpu
from jax.sharding import Mesh, PartitionSpec as P

F32, F16, BF16 = jnp.float32, jnp.float16, jnp.bfloat16
HIGH = lax.Precision.HIGH


def exponent(largest):
    return jnp.floor(jnp.log(jnp.clip(largest, 1e-30, 1e38)) * 1.4426950408889634)


def dot_t(a, b, **kw):
    return lax.dot_general(a, b, (((1,), (1,)), ((), ())), preferred_element_type=F32, **kw)


def spread(v, axis):
    n = lax.axis_size(axis)
    return lax.all_to_all(jnp.broadcast_to(v[None], (n,) + v.shape), axis, 0, 0, tiled=True)


def halves(first, second):
    lane = lax.broadcasted_iota(jnp.int32, first.shape, 1)
    low = jnp.where(lane < 64, first, pltpu.roll(second, 64, 1))
    high = jnp.where(lane < 64, pltpu.roll(first, 64, 1), second)
    return low, high


def pack_kernel(cols, s_ref, a_ref, packed_ref):
    rows, ns = s_ref.shape
    nf = a_ref.shape[1]

    def put(at, value):
        top = value.astype(BF16)
        packed_ref[0, :, at : at + value.shape[1]] = top
        low = (value - top.astype(F32)).astype(BF16)
        packed_ref[1, :, at : at + value.shape[1]] = low

    total = jnp.zeros((rows, 128), F32)
    for at in range(0, ns, 128):
        value = s_ref[:, at : at + 128]
        total = total + jnp.abs(value)
        put(at, value)
    a_own = a_ref[...]
    bound_a = jnp.max(jnp.abs(a_own), axis=1, keepdims=True)
    bound = 0.125 * jnp.sum(total, axis=1, keepdims=True) + 0.75 * nf * bound_a
    lane = lax.broadcasted_iota(jnp.int32, (rows, nf), 1)
    exps = jnp.where(lane == 0, exponent(bound), exponent(0.125 * cols * bound_a)) + 2
    put(ns, jnp.concatenate([a_own, exps], axis=1))


def turn_kernel(nx, nz, in_ref, out_ref):
    run = 128

    @pl.loop(0, in_ref.shape[0] // 64)
    def _(step):
        at_rows = pl.ds(pl.multiple_of(step * 64, 64), 64)
        for q in range(nx // 2):
            for k in range(nz // 2):
                first = (q * nz + k) * run
                second = first + nz // 2 * run
                pair = halves(
                    in_ref[at_rows, first : first + run].astype(F32),
                    in_ref[at_rows, second : second + run].astype(F32),
                )
                for h, value in enumerate(pair):
                    at = ((2 * k + h) * nx // 2 + q) * run
                    out_ref[at_rows, at : at + run] = value.astype(BF16)


def place_kernel(iz_ref, tails_ref, out_ref):
    rows, run = tails_ref.shape[2:]
    lane = lax.broadcasted_iota(jnp.int32, (rows, run), 1)
    odd = lax.rem(iz_ref[0], 2)
    for x in range(tails_ref.shape[0]):
        top = tails_ref[x, 0].astype(F32)
        low = pltpu.roll(tails_ref[x, 1].astype(F32), run // 2, 1)
        both = jnp.where(lane < run // 2, top, low)
        out_ref[x, :rows] = jnp.where(odd == 0, both, 0.0).astype(BF16)
        out_ref[x, rows:] = jnp.where(odd == 1, both, 0.0).astype(BF16)


def cross_kernel(nx, nz, at_ref, exps_ref, c_ref, place_ref, term_ref, *refs):
    block_refs, (out_ref, s_ref) = refs[:nx], refs[nx:]
    rows, ns = s_ref.shape[2:]
    for by, block_ref in enumerate(block_refs):
        s_ref[lax.rem(at_ref[0] + by, nx)] = block_ref[:, :, :ns]
    all_rows = c_ref.shape[0]
    nf = place_ref.shape[2] // 2
    run = 2 * rows
    lane = lax.broadcasted_iota(jnp.int32, (all_rows, run), 1)
    for q in range(nx // 2):
        block = s_ref[2 * q : 2 * q + 2].reshape(2 * run, ns)
        both = dot_t(c_ref[...], block)
        first, second = both[:, :run], both[:, run:]
        first = first + pltpu.roll(first, rows, 1)
        second = second + pltpu.roll(second, rows, 1)
        cross = jnp.where(lane < rows, first, second)
        at = slice(q * run, (q + 1) * run)
        out_ref[:, at] = (cross + term_ref[:, at]) * exps_ref[2]
    pair = at_ref[1] // 2
    share = jnp.zeros((all_rows, 2 * nf), F32)
    for x in range(nx):
        at = pl.ds(pl.multiple_of(x * nz * rows + pair * run, run), run)
        share += jnp.dot(c_ref[:, at], place_ref[x], preferred_element_type=F32)
    share = (share + pltpu.roll(share, nf, 1)) * exps_ref[3]
    marks = jnp.where(lane == nf, exps_ref[0], exps_ref[1])
    out_ref[:, nx * rows :] = jnp.where(lane < nf, share, marks)


def diag_kernel(top_ref, low_ref, c_ref, out_ref, parts_ref):
    nx, nz, rows, cols = top_ref.shape
    for part, v_ref in enumerate((top_ref, low_ref)):
        for z in range(nz):
            value = v_ref[:, z].reshape(nx * rows, cols)
            parts_ref[part, :, z * cols : (z + 1) * cols] = value
    for at in range(0, c_ref.shape[0], 256):
        c = c_ref[at : at + 256, :]
        both = dot_t(parts_ref[0], c) + dot_t(parts_ref[1], c)
        out_ref[:, :, at : at + 256] = both.reshape(nx, rows, 256)


def natural_kernel(nx, nz, in_ref, out_ref):
    rows = out_ref.shape[0]
    run = 2 * rows
    for q in range(nx // 2):
        for k in range(nz // 2):
            cut = slice(q * run, (q + 1) * run)
            pair = halves(in_ref[2 * k, :, cut], in_ref[2 * k + 1, :, cut])
            for h, value in enumerate(pair):
                at = ((2 * q + h) * nz // 2 + k) * run
                out_ref[:, at : at + run] = value


def shards(coupling, arrow_link, local_cov, boundary_cov, boundary_arrow, fixed_cov):
    c_own, link, local = coupling[0], arrow_link[0], local_cov[0]
    s_own, a_own = boundary_cov[0], boundary_arrow[0]
    nx, nz = lax.axis_size("x"), lax.axis_size("z")
    steps = lax.axis_size("y") * lax.axis_size("c")
    group = nx * nz
    rows, ns = c_own.shape
    nf = a_own.shape[1]
    cols = nx * rows
    ix, iz = lax.axis_index("x"), lax.axis_index("z")

    route = [(t * group + b, (t - 1) * group + b) for t in range(1, steps) for b in range(group)]
    s_own, a_own = lax.ppermute((s_own, a_own), ("y", "c", "x", "z"), route)
    packed = pl.pallas_call(
        functools.partial(pack_kernel, cols),
        out_shape=jax.ShapeDtypeStruct((2, rows, ns + 2 * nf), BF16),
        compiler_params=pltpu.CompilerParams(vmem_limit_bytes=4 << 20),
    )(s_own, a_own)
    blocks = [packed]
    for by in range(1, nx):
        blocks.append(lax.ppermute(packed, "x", [((i + by) % nx, i) for i in range(nx)]))
    tails = jnp.stack([block[..., ns:] for block in blocks] * 2)
    tails = lax.dynamic_slice_in_dim(tails, (nx - ix) % nx, nx, 0)
    a_two = tails[..., :nf]
    exps = jnp.max(tails[:, 0, :, nf : nf + 2].astype(F32), axis=(0, 1))
    exps = jnp.concatenate([exps, jnp.exp2(14 - exps)])

    link_rows = lax.dynamic_slice_in_dim(link, ix * nz * rows, nz * rows, 0)
    a_cols = a_two[:, 0].astype(F32) + a_two[:, 1].astype(F32)
    term = dot_t(link_rows, a_cols.reshape(cols, nf), precision=HIGH)
    in_smem, in_vmem = pl.BlockSpec(memory_space=pltpu.SMEM), pl.BlockSpec(memory_space=pltpu.VMEM)
    place = pl.pallas_call(
        place_kernel,
        out_shape=jax.ShapeDtypeStruct((nx, 2 * rows, 2 * nf), BF16),
        in_specs=[in_smem, in_vmem],
        compiler_params=pltpu.CompilerParams(vmem_limit_bytes=2 << 20),
    )(iz.reshape(1), tails)

    c_rows = spread(c_own, "z").reshape(nz * rows, ns)
    sent = pl.pallas_call(
        functools.partial(cross_kernel, nx, nz),
        out_shape=jax.ShapeDtypeStruct((nz * rows, cols + 2 * nf), F32),
        in_specs=[in_smem] * 2 + [in_vmem] * (3 + nx),
        scratch_shapes=[pltpu.VMEM((nx, 2, rows, ns), BF16)],
        compiler_params=pltpu.CompilerParams(vmem_limit_bytes=12 << 20),
    )(jnp.stack([ix, iz]), exps, c_rows, place, term, *blocks)
    c_turned = pl.pallas_call(
        functools.partial(turn_kernel, nx, nz),
        out_shape=jax.ShapeDtypeStruct(c_rows.shape, BF16),
        cost_estimate=pl.CostEstimate(flops=0, bytes_accessed=20 << 20, transcendentals=0),
        compiler_params=pltpu.CompilerParams(vmem_limit_bytes=6 << 20),
    )(c_rows)
    sent = sent.reshape(nz, rows, cols + 2 * nf)
    sent = sent.astype(F16)
    sent = lax.all_to_all(sent, "z", 0, 0, tiled=True)
    cross = sent[..., :cols]
    marks = sent[:, :1, cols + nf : cols + nf + 2].astype(F32)
    scale = jnp.exp2(marks[..., :1] - 14)

    every = spread(cross, "x").astype(F32) * scale[None]
    every_top = lax.reduce_precision(every, 8, 7)
    every_low = (every - every_top).astype(BF16)
    diag = pl.pallas_call(
        diag_kernel,
        out_shape=jax.ShapeDtypeStruct((nx, rows, nz * rows), F32),
        scratch_shapes=[pltpu.VMEM((2, cols, ns), BF16)],
        compiler_params=pltpu.CompilerParams(vmem_limit_bytes=10 << 20),
    )(every_top.astype(BF16), every_low, c_turned)
    diag = lax.all_to_all(diag, "x", 0, 0, tiled=True)

    cross_rows = pl.pallas_call(
        functools.partial(natural_kernel, nx, nz),
        out_shape=jax.ShapeDtypeStruct((rows, ns), F32),
        compiler_params=pltpu.CompilerParams(vmem_limit_bytes=4 << 20),
    )(cross.astype(F32) * scale)
    share = sent[..., cols : cols + nf].astype(F32) * jnp.exp2(marks[..., 1:] - 14)
    link_own = lax.dynamic_slice_in_dim(link, (ix * nz + iz) * rows, rows, 0)
    arrow = jnp.dot(link_own, fixed_cov, precision=lax.Precision.HIGHEST)
    arrow = jnp.sum(share, axis=0) + arrow
    local = lax.optimization_barrier(local + dot_t(arrow, link, precision=HIGH))
    diag_rows = local + diag.transpose(1, 0, 2).reshape(rows, ns)
    return (diag_rows[None], cross_rows[None], arrow[None])


def solution(mesh):
    mesh = Mesh(mesh.devices.reshape(8, 2, 4, 8), ("y", "c", "x", "z"))
    step, space = ("y", "c"), ("x", "z")
    row_split = P(step, space, None)
    return jax.shard_map(
        shards,
        mesh=mesh,
        in_specs=(row_split, P(step, None, None), row_split, row_split, row_split, P()),
        out_specs=(row_split, row_split, row_split),
        check_vma=False,
    )
```

```python
import functools

import jax
import jax.numpy as jnp
from jax import lax
from jax.experimental import pallas as pl
from jax.experimental.pallas import tpu as pltpu
from jax.sharding import Mesh, PartitionSpec as P

F32, F16, BF16 = jnp.float32, jnp.float16, jnp.bfloat16
HIGH = lax.Precision.HIGH


def exponent(largest):
    return jnp.floor(jnp.log(jnp.clip(largest, 1e-30, 1e38)) * 1.4426950408889634)


def dot_t(a, b, **kw):
    return lax.dot_general(a, b, (((1,), (1,)), ((), ())), preferred_element_type=F32, **kw)


def spread(v, axis):
    n = lax.axis_size(axis)
    return lax.all_to_all(jnp.broadcast_to(v[None], (n,) + v.shape), axis, 0, 0, tiled=True)


def halves(first, second):
    lane = lax.broadcasted_iota(jnp.int32, first.shape, 1)
    low = jnp.where(lane < 64, first, pltpu.roll(second, 64, 1))
    high = jnp.where(lane < 64, pltpu.roll(first, 64, 1), second)
    return low, high


def pack_kernel(cols, s_ref, a_ref, packed_ref):
    rows, ns = s_ref.shape
    nf = a_ref.shape[1]

    def put(at, value):
        top = value.astype(BF16)
        packed_ref[0, :, at : at + value.shape[1]] = top
        low = (value - top.astype(F32)).astype(BF16)
        packed_ref[1, :, at : at + value.shape[1]] = low

    total = jnp.zeros((rows, 128), F32)
    for at in range(0, ns, 128):
        value = s_ref[:, at : at + 128]
        total = total + jnp.abs(value)
        put(at, value)
    a_own = a_ref[...]
    bound_a = jnp.max(jnp.abs(a_own), axis=1, keepdims=True)
    bound = 0.125 * jnp.sum(total, axis=1, keepdims=True) + 0.75 * nf * bound_a
    lane = lax.broadcasted_iota(jnp.int32, (rows, nf), 1)
    exps = jnp.where(lane == 0, exponent(bound), exponent(0.125 * cols * bound_a)) + 2
    put(ns, jnp.concatenate([a_own, exps], axis=1))


def turn_kernel(nx, nz, in_ref, out_ref):
    run = 128

    @pl.loop(0, in_ref.shape[0] // 64)
    def _(step):
        at_rows = pl.ds(pl.multiple_of(step * 64, 64), 64)
        for q in range(nx // 2):
            for k in range(nz // 2):
                first = (q * nz + k) * run
                second = first + nz // 2 * run
                pair = halves(
                    in_ref[at_rows, first : first + run].astype(F32),
                    in_ref[at_rows, second : second + run].astype(F32),
                )
                for h, value in enumerate(pair):
                    at = ((2 * k + h) * nx // 2 + q) * run
                    out_ref[at_rows, at : at + run] = value.astype(BF16)


def place_kernel(iz_ref, tails_ref, out_ref):
    rows, run = tails_ref.shape[2:]
    lane = lax.broadcasted_iota(jnp.int32, (rows, run), 1)
    odd = lax.rem(iz_ref[0], 2)
    for x in range(tails_ref.shape[0]):
        top = tails_ref[x, 0].astype(F32)
        low = pltpu.roll(tails_ref[x, 1].astype(F32), run // 2, 1)
        both = jnp.where(lane < run // 2, top, low)
        out_ref[x, :rows] = jnp.where(odd == 0, both, 0.0).astype(BF16)
        out_ref[x, rows:] = jnp.where(odd == 1, both, 0.0).astype(BF16)


def cross_kernel(nz, iz_ref, exps_ref, c_ref, s_ref, place_ref, term_ref, out_ref):
    nx, _, rows, _ = s_ref.shape
    all_rows, ns = c_ref.shape
    nf = place_ref.shape[2] // 2
    run = 2 * rows
    lane = lax.broadcasted_iota(jnp.int32, (all_rows, run), 1)
    for q in range(nx // 2):
        block = s_ref[2 * q : 2 * q + 2, :, :, :ns].reshape(2 * run, ns)
        both = dot_t(c_ref[...], block)
        first, second = both[:, :run], both[:, run:]
        first = first + pltpu.roll(first, rows, 1)
        second = second + pltpu.roll(second, rows, 1)
        cross = jnp.where(lane < rows, first, second)
        at = slice(q * run, (q + 1) * run)
        out_ref[:, at] = (cross + term_ref[:, at]) * exps_ref[2]
    pair = iz_ref[0] // 2
    share = jnp.zeros((all_rows, 2 * nf), F32)
    for x in range(nx):
        at = pl.ds(pl.multiple_of(x * nz * rows + pair * run, run), run)
        share += jnp.dot(c_ref[:, at], place_ref[x], preferred_element_type=F32)
    share = (share + pltpu.roll(share, nf, 1)) * exps_ref[3]
    marks = jnp.where(lane == nf, exps_ref[0], exps_ref[1])
    out_ref[:, nx * rows :] = jnp.where(lane < nf, share, marks)


def diag_kernel(top_ref, low_ref, c_ref, out_ref, parts_ref):
    nx, nz, rows, cols = top_ref.shape
    for part, v_ref in enumerate((top_ref, low_ref)):
        for z in range(nz):
            value = v_ref[:, z].reshape(nx * rows, cols)
            parts_ref[part, :, z * cols : (z + 1) * cols] = value
    for at in range(0, c_ref.shape[0], 256):
        c = c_ref[at : at + 256, :]
        both = dot_t(parts_ref[0], c) + dot_t(parts_ref[1], c)
        out_ref[:, :, at : at + 256] = both.reshape(nx, rows, 256)


def natural_kernel(nx, nz, in_ref, out_ref):
    rows = out_ref.shape[0]
    run = 2 * rows
    for q in range(nx // 2):
        for k in range(nz // 2):
            cut = slice(q * run, (q + 1) * run)
            pair = halves(in_ref[2 * k, :, cut], in_ref[2 * k + 1, :, cut])
            for h, value in enumerate(pair):
                at = ((2 * q + h) * nz // 2 + k) * run
                out_ref[:, at : at + run] = value


def shards(coupling, arrow_link, local_cov, boundary_cov, boundary_arrow, fixed_cov):
    c_own, link, local = coupling[0], arrow_link[0], local_cov[0]
    s_own, a_own = boundary_cov[0], boundary_arrow[0]
    nx, nz = lax.axis_size("x"), lax.axis_size("z")
    steps = lax.axis_size("y") * lax.axis_size("c")
    group = nx * nz
    rows, ns = c_own.shape
    nf = a_own.shape[1]
    cols = nx * rows
    ix, iz = lax.axis_index("x"), lax.axis_index("z")

    route = [(t * group + b, (t - 1) * group + b) for t in range(1, steps) for b in range(group)]
    copies = jnp.broadcast_to(c_own[None], (nz, rows, ns))
    copies, s_own, a_own = lax.optimization_barrier((copies, s_own, a_own))
    packed = pl.pallas_call(
        functools.partial(pack_kernel, cols),
        out_shape=jax.ShapeDtypeStruct((2, rows, ns + 2 * nf), BF16),
        compiler_params=pltpu.CompilerParams(vmem_limit_bytes=4 << 20),
    )(s_own, a_own)
    packed = lax.ppermute(packed, ("y", "c", "x", "z"), route)
    succ = jnp.zeros((nx,) + packed.shape, BF16)
    for by in range(nx):
        block = lax.ppermute(packed, "x", [((i + by) % nx, i) for i in range(nx)]) if by else packed
        succ = lax.dynamic_update_index_in_dim(succ, block, (ix + by) % nx, 0)
    tails = succ[..., ns:]
    a_two = tails[..., :nf]
    exps = jnp.max(tails[:, 0, :, nf : nf + 2].astype(F32), axis=(0, 1))
    exps = jnp.concatenate([exps, jnp.exp2(14 - exps)])

    link_rows = lax.dynamic_slice_in_dim(link, ix * nz * rows, nz * rows, 0)
    a_cols = a_two[:, 0].astype(F32) + a_two[:, 1].astype(F32)
    term = dot_t(link_rows, a_cols.reshape(cols, nf), precision=HIGH)
    in_smem, in_vmem = pl.BlockSpec(memory_space=pltpu.SMEM), pl.BlockSpec(memory_space=pltpu.VMEM)
    place = pl.pallas_call(
        place_kernel,
        out_shape=jax.ShapeDtypeStruct((nx, 2 * rows, 2 * nf), BF16),
        in_specs=[in_smem, in_vmem],
        compiler_params=pltpu.CompilerParams(vmem_limit_bytes=2 << 20),
    )(iz.reshape(1), tails)

    c_rows = lax.all_to_all(copies, "z", 0, 0, tiled=True).reshape(nz * rows, ns)
    sent = pl.pallas_call(
        functools.partial(cross_kernel, nz),
        out_shape=jax.ShapeDtypeStruct((nz * rows, cols + 2 * nf), F32),
        in_specs=[in_smem] * 2 + [in_vmem] * 4,
        compiler_params=pltpu.CompilerParams(vmem_limit_bytes=10 << 20),
    )(iz.reshape(1), exps, c_rows, succ, place, term)
    c_turned = pl.pallas_call(
        functools.partial(turn_kernel, nx, nz),
        out_shape=jax.ShapeDtypeStruct(c_rows.shape, BF16),
        cost_estimate=pl.CostEstimate(flops=0, bytes_accessed=20 << 20, transcendentals=0),
        compiler_params=pltpu.CompilerParams(vmem_limit_bytes=6 << 20),
    )(c_rows)
    sent = sent.reshape(nz, rows, cols + 2 * nf)
    sent = sent.astype(F16)
    sent = lax.all_to_all(sent, "z", 0, 0, tiled=True)
    cross = sent[..., :cols]
    marks = sent[:, :1, cols + nf : cols + nf + 2].astype(F32)
    scale = jnp.exp2(marks[..., :1] - 14)

    every = spread(cross, "x").astype(F32) * scale[None]
    every_top = lax.reduce_precision(every, 8, 7)
    every_low = (every - every_top).astype(BF16)
    diag = pl.pallas_call(
        diag_kernel,
        out_shape=jax.ShapeDtypeStruct((nx, rows, nz * rows), F32),
        scratch_shapes=[pltpu.VMEM((2, cols, ns), BF16)],
        compiler_params=pltpu.CompilerParams(vmem_limit_bytes=10 << 20),
    )(every_top.astype(BF16), every_low, c_turned)
    diag = lax.all_to_all(diag, "x", 0, 0, tiled=True)

    cross_rows = pl.pallas_call(
        functools.partial(natural_kernel, nx, nz),
        out_shape=jax.ShapeDtypeStruct((rows, ns), F32),
        compiler_params=pltpu.CompilerParams(vmem_limit_bytes=4 << 20),
    )(cross.astype(F32) * scale)
    share = sent[..., cols : cols + nf].astype(F32) * jnp.exp2(marks[..., 1:] - 14)
    link_own = lax.dynamic_slice_in_dim(link, (ix * nz + iz) * rows, rows, 0)
    arrow = jnp.dot(link_own, fixed_cov, precision=lax.Precision.HIGHEST)
    arrow = jnp.sum(share, axis=0) + arrow
    local = lax.optimization_barrier(local + dot_t(arrow, link, precision=HIGH))
    diag_rows = local + diag.transpose(1, 0, 2).reshape(rows, ns)
    return (diag_rows[None], cross_rows[None], arrow[None])


def solution(mesh):
    mesh = Mesh(mesh.devices.reshape(8, 2, 4, 8), ("y", "c", "x", "z"))
    step, space = ("y", "c"), ("x", "z")
    row_split = P(step, space, None)
    return jax.shard_map(
        shards,
        mesh=mesh,
        in_specs=(row_split, P(step, None, None), row_split, row_split, row_split, P()),
        out_specs=(row_split, row_split, row_split),
        check_vma=False,
    )
```

```python
import functools

import jax
import jax.numpy as jnp
from jax import lax
from jax.experimental import pallas as pl
from jax.experimental.pallas import tpu as pltpu
from jax.sharding import Mesh, PartitionSpec as P

F32, F16, BF16 = jnp.float32, jnp.float16, jnp.bfloat16
HIGH = lax.Precision.HIGH


def exponent(largest):
    return jnp.floor(jnp.log(jnp.clip(largest, 1e-30, 1e38)) * 1.4426950408889634)


def dot_t(a, b, **kw):
    return lax.dot_general(a, b, (((1,), (1,)), ((), ())), preferred_element_type=F32, **kw)


def spread(v, axis):
    n = lax.axis_size(axis)
    return lax.all_to_all(jnp.broadcast_to(v[None], (n,) + v.shape), axis, 0, 0, tiled=True)


def halves(first, second):
    lane = lax.broadcasted_iota(jnp.int32, first.shape, 1)
    low = jnp.where(lane < 64, first, pltpu.roll(second, 64, 1))
    high = jnp.where(lane < 64, pltpu.roll(first, 64, 1), second)
    return low, high


def copies_kernel(in_ref, out_ref):
    for z in range(out_ref.shape[0]):
        out_ref[z] = in_ref[...]


def pack_kernel(cols, s_ref, a_ref, packed_ref):
    rows, ns = s_ref.shape
    nf = a_ref.shape[1]

    def put(at, value):
        top = value.astype(BF16)
        packed_ref[0, :, at : at + value.shape[1]] = top
        low = (value - top.astype(F32)).astype(BF16)
        packed_ref[1, :, at : at + value.shape[1]] = low

    total = jnp.zeros((rows, 128), F32)
    for at in range(0, ns, 128):
        value = s_ref[:, at : at + 128]
        total = total + jnp.abs(value)
        put(at, value)
    a_own = a_ref[...]
    bound_a = jnp.max(jnp.abs(a_own), axis=1, keepdims=True)
    bound = 0.125 * jnp.sum(total, axis=1, keepdims=True) + 0.75 * nf * bound_a
    lane = lax.broadcasted_iota(jnp.int32, (rows, nf), 1)
    exps = jnp.where(lane == 0, exponent(bound), exponent(0.125 * cols * bound_a)) + 2
    put(ns, jnp.concatenate([a_own, exps], axis=1))


def turn_kernel(nx, nz, in_ref, out_ref):
    run = 128

    @pl.loop(0, in_ref.shape[0] // 64)
    def _(step):
        at_rows = pl.ds(pl.multiple_of(step * 64, 64), 64)
        for q in range(nx // 2):
            for k in range(nz // 2):
                first = (q * nz + k) * run
                second = first + nz // 2 * run
                pair = halves(
                    in_ref[at_rows, first : first + run].astype(F32),
                    in_ref[at_rows, second : second + run].astype(F32),
                )
                for h, value in enumerate(pair):
                    at = ((2 * k + h) * nx // 2 + q) * run
                    out_ref[at_rows, at : at + run] = value.astype(BF16)


def place_kernel(iz_ref, tails_ref, out_ref):
    rows, run = tails_ref.shape[2:]
    lane = lax.broadcasted_iota(jnp.int32, (rows, run), 1)
    odd = lax.rem(iz_ref[0], 2)
    for x in range(tails_ref.shape[0]):
        top = tails_ref[x, 0].astype(F32)
        low = pltpu.roll(tails_ref[x, 1].astype(F32), run // 2, 1)
        both = jnp.where(lane < run // 2, top, low)
        out_ref[x, :rows] = jnp.where(odd == 0, both, 0.0).astype(BF16)
        out_ref[x, rows:] = jnp.where(odd == 1, both, 0.0).astype(BF16)


def cross_kernel(nx, nz, at_ref, exps_ref, c_ref, place_ref, term_ref, *refs):
    block_refs, (out_ref, s_ref) = refs[:nx], refs[nx:]
    rows, ns = s_ref.shape[2:]
    for by, block_ref in enumerate(block_refs):
        s_ref[lax.rem(at_ref[0] + by, nx)] = block_ref[:, :, :ns]
    all_rows = c_ref.shape[0]
    nf = place_ref.shape[2] // 2
    run = 2 * rows
    lane = lax.broadcasted_iota(jnp.int32, (all_rows, run), 1)
    for q in range(nx // 2):
        block = s_ref[2 * q : 2 * q + 2].reshape(2 * run, ns)
        both = dot_t(c_ref[...], block)
        first, second = both[:, :run], both[:, run:]
        first = first + pltpu.roll(first, rows, 1)
        second = second + pltpu.roll(second, rows, 1)
        cross = jnp.where(lane < rows, first, second)
        at = slice(q * run, (q + 1) * run)
        out_ref[:, at] = (cross + term_ref[:, at]) * exps_ref[2]
    pair = at_ref[1] // 2
    share = jnp.zeros((all_rows, 2 * nf), F32)
    for x in range(nx):
        at = pl.ds(pl.multiple_of(x * nz * rows + pair * run, run), run)
        share += jnp.dot(c_ref[:, at], place_ref[x], preferred_element_type=F32)
    share = (share + pltpu.roll(share, nf, 1)) * exps_ref[3]
    marks = jnp.where(lane == nf, exps_ref[0], exps_ref[1])
    out_ref[:, nx * rows :] = jnp.where(lane < nf, share, marks)


def diag_kernel(top_ref, low_ref, c_ref, out_ref, parts_ref):
    nx, nz, rows, cols = top_ref.shape
    for part, v_ref in enumerate((top_ref, low_ref)):
        for z in range(nz):
            value = v_ref[:, z].reshape(nx * rows, cols)
            parts_ref[part, :, z * cols : (z + 1) * cols] = value
    for at in range(0, c_ref.shape[0], 256):
        c = c_ref[at : at + 256, :]
        both = dot_t(parts_ref[0], c) + dot_t(parts_ref[1], c)
        out_ref[:, :, at : at + 256] = both.reshape(nx, rows, 256)


def natural_kernel(nx, nz, in_ref, out_ref):
    rows = out_ref.shape[0]
    run = 2 * rows
    for q in range(nx // 2):
        for k in range(nz // 2):
            cut = slice(q * run, (q + 1) * run)
            pair = halves(in_ref[2 * k, :, cut], in_ref[2 * k + 1, :, cut])
            for h, value in enumerate(pair):
                at = ((2 * q + h) * nz // 2 + k) * run
                out_ref[:, at : at + run] = value


def shards(coupling, arrow_link, local_cov, boundary_cov, boundary_arrow, fixed_cov):
    c_own, link, local = coupling[0], arrow_link[0], local_cov[0]
    s_own, a_own = boundary_cov[0], boundary_arrow[0]
    nx, nz = lax.axis_size("x"), lax.axis_size("z")
    steps = lax.axis_size("y") * lax.axis_size("c")
    group = nx * nz
    rows, ns = c_own.shape
    nf = a_own.shape[1]
    cols = nx * rows
    ix, iz = lax.axis_index("x"), lax.axis_index("z")

    route = [(t * group + b, (t - 1) * group + b) for t in range(1, steps) for b in range(group)]
    s_own, a_own = lax.ppermute((s_own, a_own), ("y", "c", "x", "z"), route)
    packed = pl.pallas_call(
        functools.partial(pack_kernel, cols),
        out_shape=jax.ShapeDtypeStruct((2, rows, ns + 2 * nf), BF16),
        compiler_params=pltpu.CompilerParams(vmem_limit_bytes=4 << 20),
    )(s_own, a_own)
    blocks = [packed]
    for by in range(1, nx):
        blocks.append(lax.ppermute(packed, "x", [((i + by) % nx, i) for i in range(nx)]))
    tails = jnp.stack([block[..., ns:] for block in blocks] * 2)
    tails = lax.dynamic_slice_in_dim(tails, (nx - ix) % nx, nx, 0)
    a_two = tails[..., :nf]
    exps = jnp.max(tails[:, 0, :, nf : nf + 2].astype(F32), axis=(0, 1))
    exps = jnp.concatenate([exps, jnp.exp2(14 - exps)])

    link_rows = lax.dynamic_slice_in_dim(link, ix * nz * rows, nz * rows, 0)
    a_cols = a_two[:, 0].astype(F32) + a_two[:, 1].astype(F32)
    term = dot_t(link_rows, a_cols.reshape(cols, nf), precision=HIGH)
    in_smem, in_vmem = pl.BlockSpec(memory_space=pltpu.SMEM), pl.BlockSpec(memory_space=pltpu.VMEM)
    place = pl.pallas_call(
        place_kernel,
        out_shape=jax.ShapeDtypeStruct((nx, 2 * rows, 2 * nf), BF16),
        in_specs=[in_smem, in_vmem],
        compiler_params=pltpu.CompilerParams(vmem_limit_bytes=2 << 20),
    )(iz.reshape(1), tails)

    copies = pl.pallas_call(
        copies_kernel,
        out_shape=jax.ShapeDtypeStruct((nz, rows, ns), BF16),
        compiler_params=pltpu.CompilerParams(vmem_limit_bytes=56 << 20),
    )(c_own)
    c_rows = lax.all_to_all(copies, "z", 0, 0, tiled=True).reshape(nz * rows, ns)
    sent = pl.pallas_call(
        functools.partial(cross_kernel, nx, nz),
        out_shape=jax.ShapeDtypeStruct((nz * rows, cols + 2 * nf), F32),
        in_specs=[in_smem] * 2 + [in_vmem] * (3 + nx),
        scratch_shapes=[pltpu.VMEM((nx, 2, rows, ns), BF16)],
        compiler_params=pltpu.CompilerParams(vmem_limit_bytes=12 << 20),
    )(jnp.stack([ix, iz]), exps, c_rows, place, term, *blocks)
    c_turned = pl.pallas_call(
        functools.partial(turn_kernel, nx, nz),
        out_shape=jax.ShapeDtypeStruct(c_rows.shape, BF16),
        cost_estimate=pl.CostEstimate(flops=0, bytes_accessed=20 << 20, transcendentals=0),
        compiler_params=pltpu.CompilerParams(vmem_limit_bytes=6 << 20),
    )(c_rows)
    sent = sent.reshape(nz, rows, cols + 2 * nf)
    sent = sent.astype(F16)
    sent = lax.all_to_all(sent, "z", 0, 0, tiled=True)
    cross = sent[..., :cols]
    marks = sent[:, :1, cols + nf : cols + nf + 2].astype(F32)
    scale = jnp.exp2(marks[..., :1] - 14)

    every = spread(cross, "x").astype(F32) * scale[None]
    every_top = lax.reduce_precision(every, 8, 7)
    every_low = (every - every_top).astype(BF16)
    diag = pl.pallas_call(
        diag_kernel,
        out_shape=jax.ShapeDtypeStruct((nx, rows, nz * rows), F32),
        scratch_shapes=[pltpu.VMEM((2, cols, ns), BF16)],
        compiler_params=pltpu.CompilerParams(vmem_limit_bytes=10 << 20),
    )(every_top.astype(BF16), every_low, c_turned)
    diag = lax.all_to_all(diag, "x", 0, 0, tiled=True)

    cross_rows = pl.pallas_call(
        functools.partial(natural_kernel, nx, nz),
        out_shape=jax.ShapeDtypeStruct((rows, ns), F32),
        compiler_params=pltpu.CompilerParams(vmem_limit_bytes=4 << 20),
    )(cross.astype(F32) * scale)
    share = sent[..., cols : cols + nf].astype(F32) * jnp.exp2(marks[..., 1:] - 14)
    link_own = lax.dynamic_slice_in_dim(link, (ix * nz + iz) * rows, rows, 0)
    arrow = jnp.dot(link_own, fixed_cov, precision=lax.Precision.HIGHEST)
    arrow = jnp.sum(share, axis=0) + arrow
    local = lax.optimization_barrier(local + dot_t(arrow, link, precision=HIGH))
    diag_rows = local + diag.transpose(1, 0, 2).reshape(rows, ns)
    return (diag_rows[None], cross_rows[None], arrow[None])


def solution(mesh):
    mesh = Mesh(mesh.devices.reshape(8, 2, 4, 8), ("y", "c", "x", "z"))
    step, space = ("y", "c"), ("x", "z")
    row_split = P(step, space, None)
    return jax.shard_map(
        shards,
        mesh=mesh,
        in_specs=(row_split, P(step, None, None), row_split, row_split, row_split, P()),
        out_specs=(row_split, row_split, row_split),
        check_vma=False,
    )
```
